32 devices in a mesh: groups: 2 (over y), fsdp: 4 (over z), tp: 2 (over x), sub: 2 (over core).
Axes of the slice: x: 2, y: 2, z: 4, core: 2. Of those that a mesh axis runs over, the one named last changes fastest.
Arguments:
- activations: bfloat16 [8192, 8192], P(('groups', 'fsdp', 'sub'), 'tp'), parts along dimension 0, may hold values from -6 to 6
- output_gradient: bfloat16 [8192, 2048], P(('groups', 'fsdp', 'sub'), 'tp'), parts along dimension 0, may hold values from -4 to 4
- base_weight: bfloat16 [8192, 2048], P('tp', 'fsdp'), may hold values from -0.0625 to 0.0625
- factor_down: bfloat16 [128, 16, 8192], P(('groups', 'fsdp', 'sub'), None, 'tp'), parts along dimension 0, may hold values from -0.0625 to 0.0625
- factor_up: bfloat16 [128, 16, 2048], P(('groups', 'fsdp', 'sub'), None, 'tp'), parts along dimension 0, may hold values from -1.5 to 1.5
- counts: int32 [16, 64], P(('groups', 'fsdp', 'sub')), parts along dimension 0, may hold values from 1 to 64, 512 in all within a row
- owners: int32 [128], P('groups'), parts along dimension 0, may hold values from 0 to 63, each once
Outputs:
- input_gradient: bfloat16 [8192, 8192], P(('groups', 'fsdp', 'sub'), 'tp'), parts along dimension 0
- grad_down: float32 [128, 16, 8192], P(('groups', 'fsdp', 'sub'), None, 'tp'), parts along dimension 0
- up_factor_gradient: float32 [128, 16, 2048], P(('groups', 'fsdp', 'sub'), None, 'tp'), parts along dimension 0
The draws below stay inside these ranges and needn't reach their ends.
There are 2 independent parts, one for each index of `groups`. The reference program is written for one: setup_inputs(seed, part) draws one part's arguments, and reference() takes and returns one part's arrays. A program takes and returns all parts, laid end to end along the dimension named above; an argument that names none is the same for every part. Nothing has to cross between parts.
Inputs may be any that keep to these rules, and one draw needn't show every extreme that they name: `counts`: each row sums to 512; every adapter has tokens in every block, and some adapter has exactly 64 in a block. `owners`: a permutation of the slots.
All inputs are finite; a program needn't handle non-finite values.
Results may differ from the reference program's by a relative error of at most 0.013.
Values may be sent and summed in bfloat16 or wider, within the bound.
No kernel may reach another device: no remote copies, remote signals or barrier semaphores. Data moves between devices by JAX's collectives and lax.ppermute only.
A program may use at most 256 MiB of HBM per device.

```python
import math
import jax
import jax.numpy as jnp
import numpy as np
from jax import lax

D = 8192
KV2 = 2048
RANK = 16
ADAPTERS = 64
TOK_DEV = 512
BLOCKS = 8
TOKENS = 4096


def shard_levels(own_key, shape, pieces, low, high):
    def one(axis_at, parts):
        steps = jax.random.uniform(jax.random.fold_in(jax.random.fold_in(own_key, 6), axis_at), (parts,), jnp.float32, low / len(pieces), high / len(pieces))
        return jnp.repeat(jnp.exp(steps), shape[axis_at] // parts).reshape((-1,) + (1,) * (len(shape) - axis_at - 1))

    loudness = one(*pieces[0])
    for cut in pieces[1:]:
        loudness = loudness * one(*cut)
    return loudness


def profile(count, total, limit, slope):
    portions = [(1 << 20) // math.isqrt(standing ** slope) + 1 for standing in range(2, count + 1)]
    rest, given = total - limit - (count - 1), [1] * (count - 1)
    while rest > 0:
        candidates = [i for i in range(count - 1) if given[i] < limit]
        whole, budget = sum([portions[i] for i in candidates]), rest
        for i in candidates:
            addition = min(limit - given[i], max(1, budget * portions[i] // whole), rest)
            given[i] = given[i] + addition
            rest = rest - addition
    return np.array([limit] + given)


def ragged_sizes(rng, number_of, total, limit, slope):
    if number_of == 2:
        one = jax.random.randint(rng, (), max(1, total - limit), min(limit, total - 1) + 1)
        return jnp.stack([one, total - one])
    sizes = jnp.asarray(profile(number_of, total, limit, slope), jnp.int32)
    couples = (number_of - 1) // 2
    donor, receiver = sizes[1:1 + 2 * couples:2], sizes[2:2 + 2 * couples:2]
    margin = jnp.minimum(donor - 1, limit - receiver)
    moved = jax.random.randint(jax.random.fold_in(rng, 1), (couples,), 0, 1 << 20) % (margin + 1)
    sizes = sizes.at[1:1 + 2 * couples:2].set(donor - moved).at[2:2 + 2 * couples:2].set(receiver + moved)
    return sizes[jax.random.permutation(jax.random.fold_in(rng, 2), number_of)]


def normal_values(own_key, extent, spread, bound, pieces=(), kind=jnp.bfloat16):
    drawn = spread * jax.random.normal(own_key, extent, jnp.float32)
    if pieces:
        drawn = drawn * shard_levels(own_key, extent, pieces, -0.22, 0.18)
    return jnp.clip(drawn, -bound, bound).astype(kind)


def setup_inputs(seed: int = 0, part: int = 0) -> dict:
    key_list = jax.random.split(jax.random.key(seed), 8)
    part_keys = jax.random.split(jax.random.fold_in(key_list[7], part), 8)
    activations = normal_values(part_keys[0], (TOKENS, D), 1.0, 6.0, ((0, 8), (1, 2)))
    output_gradient = normal_values(part_keys[1], (TOKENS, KV2), 0.25, 4.0, ((0, 8), (1, 2)))
    base_weight = normal_values(key_list[2], (D, KV2), D ** -0.5, 0.0625, ((0, 2), (1, 4)))
    factor_down = normal_values(part_keys[3], (ADAPTERS, RANK, D), D ** -0.5, 0.0625, ((0, 8), (2, 2)))
    factor_up = normal_values(part_keys[4], (ADAPTERS, RANK, KV2), RANK ** -0.5, 1.5, ((0, 8), (2, 2)))
    counts = jax.vmap(lambda own: ragged_sizes(own, ADAPTERS, TOK_DEV, TOK_DEV // 8, 2))(jax.random.split(part_keys[5], BLOCKS)).reshape((BLOCKS, ADAPTERS)).astype(jnp.int32)
    owners = jax.random.permutation(part_keys[6], ADAPTERS).astype(jnp.int32)
    return {"activations": activations, "output_gradient": output_gradient, "base_weight": base_weight, "factor_down": factor_down, "factor_up": factor_up, "counts": counts, "owners": owners}


adapter_scale_factor = 0.25


def reference(activations, output_gradient, base_weight, factor_down, factor_up, counts, owners):
    total = activations.shape[0]
    seg_ends = jnp.cumsum(counts, axis=1).astype(jnp.int32)
    seg_starts = seg_ends - counts
    token_index = jnp.arange(total, dtype=jnp.int32)
    block_row = token_index // TOK_DEV
    position = (token_index % TOK_DEV)[:, None]
    row_starts = seg_starts[block_row]
    row_ends = seg_ends[block_row]
    adapter_hot = ((position >= row_starts) & (position < row_ends)).astype(jnp.float32)
    slot_ids = jnp.arange(ADAPTERS, dtype=jnp.int32)
    owner_hot = (owners[:, None] == slot_ids[None, :]).astype(jnp.float32)
    slot_onehot_matrix = jnp.dot(adapter_hot, owner_hot, precision=lax.Precision.HIGHEST)
    down_flattened = jnp.transpose(factor_down, (2, 0, 1)).reshape(D, ADAPTERS * RANK)
    up_flat = jnp.transpose(factor_up, (2, 0, 1)).reshape(KV2, ADAPTERS * RANK)
    low_all = jnp.dot(activations, down_flattened, preferred_element_type=jnp.float32).reshape(total, ADAPTERS, RANK)
    low_in = jnp.sum(low_all * slot_onehot_matrix[:, :, None], axis=1)
    backward_everything = jnp.dot(output_gradient, up_flat, preferred_element_type=jnp.float32).reshape(total, ADAPTERS, RANK)
    narrow_backward = adapter_scale_factor * jnp.sum(backward_everything * slot_onehot_matrix[:, :, None], axis=1)
    broad_backward = (slot_onehot_matrix[:, :, None] * narrow_backward[:, None, :]).astype(jnp.bfloat16).reshape(total, ADAPTERS * RANK)
    broad_input = (slot_onehot_matrix[:, :, None] * low_in[:, None, :]).astype(jnp.bfloat16).reshape(total, ADAPTERS * RANK)
    frozen_contribution = jnp.dot(output_gradient, base_weight.T, preferred_element_type=jnp.float32)
    adapter_contribution = jnp.dot(broad_backward, down_flattened.T, preferred_element_type=jnp.float32)
    input_gradient = (frozen_contribution + adapter_contribution).astype(jnp.bfloat16)
    grad_down = jnp.dot(broad_backward.T, activations, preferred_element_type=jnp.float32)
    grad_down = grad_down.reshape(ADAPTERS, RANK, D)
    up_factor_gradient = adapter_scale_factor * jnp.dot(broad_input.T, output_gradient, preferred_element_type=jnp.float32)
    up_factor_gradient = up_factor_gradient.reshape(ADAPTERS, RANK, KV2)
    return input_gradient, grad_down, up_factor_gradient
```

```python
import jax
import jax.numpy as jnp
from jax import lax
from jax.sharding import PartitionSpec as P

adapter_scale_factor = 0.25


def local(activations, output_gradient, base_weight, factor_down, factor_up, counts, owners):
    tok_rows = activations.shape[0]
    adapter_count = owners.shape[0]
    seg_ends = jnp.cumsum(counts[0])
    seg_starts = seg_ends - counts[0]
    position = lax.broadcasted_iota(jnp.int32, (tok_rows, adapter_count), 0)
    adapter_hot = ((position >= seg_starts[None, :]) & (position < seg_ends[None, :])).astype(
        jnp.float32
    )
    slot_grid = lax.broadcasted_iota(jnp.int32, (adapter_count, adapter_count), 1)
    owner_hot = (owners[:, None] == slot_grid).astype(jnp.float32)
    slot_onehot_matrix = jnp.dot(adapter_hot, owner_hot, precision=lax.Precision.HIGHEST)
    down_projected_every, up_all = (
        lax.all_gather(factor_down, ("fsdp", "sub"), axis=0, tiled=True),
        lax.all_gather(factor_up, ("fsdp", "sub"), axis=0, tiled=True),
    )
    grad_full = lax.all_gather(output_gradient, "tp", axis=1, tiled=True)
    low_part = jnp.einsum(
        "td,grd->tgr", activations, down_projected_every, preferred_element_type=jnp.float32
    )
    back_part = jnp.einsum(
        "tc,grc->tgr", output_gradient, up_all, preferred_element_type=jnp.float32
    )
    low_sel = jnp.sum(low_part * slot_onehot_matrix[:, :, None], axis=1)
    back_sel = jnp.sum(back_part * slot_onehot_matrix[:, :, None], axis=1)
    low_in, backward_total = (
        lax.psum(low_sel.astype(jnp.bfloat16), "tp").astype(jnp.float32),
        lax.psum(back_sel.astype(jnp.bfloat16), "tp").astype(jnp.float32),
    )
    narrow_backward = adapter_scale_factor * backward_total
    broad_backward = (slot_onehot_matrix[:, :, None] * narrow_backward[:, None, :]).astype(
        jnp.bfloat16
    )
    broad_input = (slot_onehot_matrix[:, :, None] * low_in[:, None, :]).astype(jnp.bfloat16)
    adapter_contribution = jnp.einsum(
        "psl,sln->pn", broad_backward, down_projected_every, preferred_element_type=jnp.float32
    )
    copies = lax.axis_size("groups") * lax.axis_size("sub")
    part = lax.axis_index("groups") * lax.axis_size("sub") + lax.axis_index("sub")
    rows = base_weight.shape[0] // copies
    own_rows = lax.dynamic_slice_in_dim(base_weight, part * rows, rows, axis=0)
    weight = lax.all_gather(own_rows, ("fsdp", "groups", "sub"), axis=0, tiled=True)
    shards = lax.axis_size("fsdp")
    width = base_weight.shape[1]
    weight = weight.reshape(shards, copies * rows, width)
    reduced_total = adapter_contribution + jnp.einsum(
        "tfc,fdc->td",
        grad_full.reshape(tok_rows, shards, width),
        weight,
        preferred_element_type=jnp.float32,
    )
    input_gradient = reduced_total.astype(jnp.bfloat16)
    down_partial = jnp.einsum(
        "tgr,td->grd", broad_backward, activations, preferred_element_type=jnp.float32
    )
    up_factor_pieces = adapter_scale_factor * jnp.einsum(
        "tgr,tc->grc", broad_input, output_gradient, preferred_element_type=jnp.float32
    )
    grad_down, up_factor_gradient = (
        lax.psum_scatter(
            piece.astype(jnp.bfloat16), ("fsdp", "sub"), scatter_dimension=0, tiled=True
        ).astype(jnp.float32)
        for piece in (down_partial, up_factor_pieces)
    )
    return (input_gradient, grad_down, up_factor_gradient)


def solution(mesh):
    placed = (
        P(("groups", "fsdp", "sub"), "tp"),
        P(("groups", "fsdp", "sub"), "tp"),
        P("tp", "fsdp"),
        P(("groups", "fsdp", "sub"), None, "tp"),
        P(("groups", "fsdp", "sub"), None, "tp"),
        P(("groups", "fsdp", "sub"), None),
        P("groups"),
    )
    return jax.shard_map(
        local,
        mesh=mesh,
        in_specs=placed,
        out_specs=(
            P(("groups", "fsdp", "sub"), "tp"),
            P(("groups", "fsdp", "sub"), None, "tp"),
            P(("groups", "fsdp", "sub"), None, "tp"),
        ),
        check_vma=False,
    )
```

```python
import functools

import jax
import jax.numpy as jnp
from jax import lax
from jax.experimental import pallas as pl
from jax.experimental.pallas import tpu as pltpu
from jax.sharding import PartitionSpec as P

adapter_scale_factor = 0.25
F32 = jnp.float32
BF16 = jnp.bfloat16
SLOT_AXES = ("fsdp", "sub")


def around(axis):
    count = lax.axis_size(axis)
    return [(i, (i + 1) % count) for i in range(count)]


def line_gather(own):
    count = lax.axis_size("fsdp")
    up, down = [own], [own]
    for step in range(1, count):
        up.append(lax.ppermute(up[-1], "fsdp", [(i, i + 1) for i in range(step - 1, count - 1)]))
        down.append(lax.ppermute(down[-1], "fsdp", [(i, i - 1) for i in range(1, count - step + 1)]))
    return up, down


def in_arrival_order(up, down):
    count, at = lax.axis_size("fsdp"), lax.axis_index("fsdp")
    arrived, whose = [], []
    for step in range(1, count):
        pick, owner = None, 0
        for z in range(count):
            if 2 * z >= count:
                from_up, far = (True, step) if step <= z else (False, step - z)
            else:
                room = count - 1 - z
                from_up, far = (False, step) if step <= room else (True, step - room)
            one = up[far] if from_up else down[far]
            pick = one if pick is None else jnp.where(at == z, one, pick)
            owner = jnp.where(at == z, z - far if from_up else z + far, owner)
        arrived.append(pick)
        whose.append(owner)
    return arrived, whose


def line_scatter_sum(blocks):
    count = lax.axis_size("fsdp")
    from_above = from_below = None
    for step in range(1, count):
        lower = blocks[count - step] if from_above is None else blocks[count - step] + from_above
        upper = blocks[step] if from_below is None else blocks[step] + from_below
        from_above = lax.ppermute(
            lower.astype(BF16), "fsdp", [(i, i - 1) for i in range(count - step, count)]
        ).astype(F32)
        from_below = lax.ppermute(
            upper.astype(BF16), "fsdp", [(i, i + 1) for i in range(step)]
        ).astype(F32)
    total = blocks[0]
    if from_above is not None:
        total = total + from_above + from_below
    return total


def sum_over_tp(part):
    if lax.axis_size("tp") == 2:
        return part + lax.ppermute(part.astype(BF16), "tp", around("tp")).astype(F32)
    return lax.psum(part.astype(BF16), "tp").astype(F32)


def input_gradient_kernel(shards, *refs):
    _, refs = refs[0], refs[1:]
    grads, weights = refs[:shards], refs[shards : 2 * shards]
    wide, factors, out = refs[2 * shards], refs[2 * shards + 1], refs[-1]
    total = jnp.dot(wide[...], factors[...], preferred_element_type=F32)
    for grad, weight in zip(grads, weights, strict=True):
        total += lax.dot_general(
            grad[...], weight[...], (((1,), (1,)), ((), ())), preferred_element_type=F32
        )
    out[...] = total.astype(out.dtype)


def input_gradient_part(scalars, grad_full, weights, wide, factors, so_far):
    tokens, features = wide.shape[0], factors.shape[1]
    shards = len(weights)
    rows, width = weights[0].shape
    block = min(rows, 512)
    steps = rows // block
    grad_spec = [
        pl.BlockSpec((tokens, width), functools.partial(lambda k, j, s: (0, s[k]), k))
        for k in range(shards)
    ]
    weight_spec = [pl.BlockSpec((block, width), lambda j, s: (j, 0)) for _ in range(shards)]
    at = lambda j, s: (0, s[shards] * steps + j)
    in_specs = (
        grad_spec
        + weight_spec
        + [
            pl.BlockSpec(wide.shape, lambda j, s: (0, 0)),
            pl.BlockSpec((factors.shape[0], block), at),
        ]
    )
    operands = [scalars] + [grad_full] * shards + list(weights) + [wide, factors]
    aliases = {}
    if so_far is not None:
        in_specs = in_specs + [pl.BlockSpec(memory_space=pl.ANY)]
        operands.append(so_far)
        aliases = {len(operands) - 1: 0}
    return pl.pallas_call(
        functools.partial(input_gradient_kernel, shards),
        grid_spec=pltpu.PrefetchScalarGridSpec(
            num_scalar_prefetch=1,
            grid=(steps,),
            in_specs=in_specs,
            out_specs=pl.BlockSpec((tokens, block), at),
        ),
        out_shape=jax.ShapeDtypeStruct((tokens, features), BF16),
        input_output_aliases=aliases,
        compiler_params=pltpu.CompilerParams(vmem_limit_bytes=32 * 2**20),
        cost_estimate=pl.CostEstimate(
            flops=2 * tokens * rows * (shards * width + wide.shape[1]),
            bytes_accessed=8 * 2**20,
            transcendentals=0,
        ),
    )(*operands)


def local(activations, output_gradient, base_weight, factor_down, factor_up, counts, owners):
    tokens, features = activations.shape
    columns = output_gradient.shape[1]
    own_slots, rank = factor_down.shape[:2]
    slots = owners.shape[0]
    n, subs = lax.axis_size("fsdp"), lax.axis_size("sub")
    groups = lax.axis_size("groups")
    z, sub, y = lax.axis_index("fsdp"), lax.axis_index("sub"), lax.axis_index("groups")

    up_all = lax.all_gather(factor_up, SLOT_AXES, axis=0, tiled=True)
    down_all = lax.all_gather(factor_down, SLOT_AXES, axis=0, tiled=True)

    copies = groups * subs
    rows, width = base_weight.shape[0] // copies, base_weight.shape[1]
    by_part = base_weight.reshape(copies, rows, width)
    own_rows = lax.dynamic_index_in_dim(by_part, y * subs + sub, 0, keepdims=False)
    arrived, whose = in_arrival_order(*line_gather(own_rows))
    weight_parts = [[] for _ in range(copies)]
    parts = [((y - a) % groups) * subs + (sub - b) % subs for b in range(subs) for a in range(groups)]
    for part, held in zip(parts, weight_parts, strict=True):
        held.append(lax.dynamic_index_in_dim(by_part, part, 0, keepdims=False))
    for mine in arrived:
        over_groups = [mine]
        for _ in range(1, groups):
            over_groups.append(lax.ppermute(over_groups[-1], "groups", around("groups")))
        both = over_groups
        for b in range(subs):
            if b:
                both = [lax.ppermute(one, "sub", around("sub")) for one in both]
            for a in range(groups):
                weight_parts[b * groups + a].append(both[a])
    shard_ids = [z] + whose

    if lax.axis_size("tp") == 2:
        other = lax.ppermute(output_gradient, "tp", around("tp"))
        first = lax.axis_index("tp") == 0
        grad_full = jnp.concatenate(
            [jnp.where(first, output_gradient, other), jnp.where(first, other, output_gradient)], axis=1
        )
    else:
        grad_full = lax.all_gather(output_gradient, "tp", axis=1, tiled=True)

    seg_ends = jnp.cumsum(counts[0])
    seg_starts = seg_ends - counts[0]
    hot = owners[:, None] == lax.broadcasted_iota(jnp.int32, (slots, slots), 1)
    starts = jnp.sum(jnp.where(hot, seg_starts[:, None], 0), axis=0)
    ends = jnp.sum(jnp.where(hot, seg_ends[:, None], 0), axis=0)
    position = lax.broadcasted_iota(jnp.int32, (tokens, slots), 0)
    mask = (position >= starts[None, :]) & (position < ends[None, :])
    by_owner_start = starts.reshape(n, subs, own_slots)
    by_owner_end = ends.reshape(n, subs, own_slots)
    line = [(z - j) % n for j in range(n)]

    def ranged(b):
        s = jnp.concatenate([by_owner_start[at, (sub + b) % subs] for at in line])
        e = jnp.concatenate([by_owner_end[at, (sub + b) % subs] for at in line])
        pos = lax.broadcasted_iota(jnp.int32, (tokens, n * own_slots), 0)
        return (pos >= s[None, :]) & (pos < e[None, :])

    back_part = jnp.einsum("tc,grc->tgr", output_gradient, up_all, preferred_element_type=F32)
    back_sel = jnp.sum(jnp.where(mask[:, :, None], back_part, 0.0), axis=1)
    low_back = adapter_scale_factor * sum_over_tp(back_sel)

    def spread(low, where):
        return jnp.where(where[:, :, None], low[:, None, :], 0.0).astype(BF16)

    pieces = None
    for b in range(subs - 1, -1, -1):
        piece = jnp.einsum(
            "tgr,td->grd", spread(low_back, ranged(b)), activations, preferred_element_type=F32
        )
        if b:
            got = lax.ppermute(piece.astype(BF16), "sub", [(i, (i + b) % subs) for i in range(subs)])
            pieces = got.astype(F32) if pieces is None else pieces + got.astype(F32)
        else:
            pieces = piece if pieces is None else piece + pieces
    grad_down = line_scatter_sum(list(pieces.reshape(n, own_slots, rank, features)))

    low_part = jnp.einsum("td,grd->tgr", activations, down_all, preferred_element_type=F32)
    low_sel = jnp.sum(jnp.where(mask[:, :, None], low_part, 0.0), axis=1)
    low_in = sum_over_tp(low_sel)
    up_pieces = adapter_scale_factor * jnp.einsum(
        "tgr,tc->grc", spread(low_in, mask), output_gradient, preferred_element_type=F32
    )
    up_factor_gradient = jnp.sum(
        lax.all_to_all(
            up_pieces[None].astype(BF16), SLOT_AXES, split_axis=1, concat_axis=0, tiled=True
        ).astype(F32),
        axis=0,
    )

    wide = spread(low_back, mask).reshape(tokens, slots * rank)
    factors = down_all.reshape(slots * rank, features)
    input_gradient = None
    for part, weights in zip(parts, weight_parts, strict=True):
        scalars = jnp.stack(shard_ids + [part]).astype(jnp.int32)
        input_gradient = input_gradient_part(
            scalars, grad_full, weights, wide, factors, input_gradient
        )
    return (input_gradient, grad_down, up_factor_gradient)


def solution(mesh):
    placed = (
        P(("groups", "fsdp", "sub"), "tp"),
        P(("groups", "fsdp", "sub"), "tp"),
        P("tp", "fsdp"),
        P(("groups", "fsdp", "sub"), None, "tp"),
        P(("groups", "fsdp", "sub"), None, "tp"),
        P(("groups", "fsdp", "sub"), None),
        P("groups"),
    )
    return jax.shard_map(
        local,
        mesh=mesh,
        in_specs=placed,
        out_specs=(
            P(("groups", "fsdp", "sub"), "tp"),
            P(("groups", "fsdp", "sub"), None, "tp"),
            P(("groups", "fsdp", "sub"), None, "tp"),
        ),
        check_vma=False,
    )
```

```python
import functools

import jax
import jax.numpy as jnp
from jax import lax
from jax.experimental import pallas as pl
from jax.experimental.pallas import tpu as pltpu
from jax.sharding import PartitionSpec as P

adapter_scale_factor = 0.25
F32 = jnp.float32
BF16 = jnp.bfloat16
LANES = 128
TRANS_B = (((1,), (1,)), ((), ()))
SMALL = pl.CostEstimate(flops=1, bytes_accessed=1, transcendentals=0)
TRANS_A = (((0,), (0,)), ((), ()))


def after(value, *earlier):
    return lax.optimization_barrier((value, *earlier))[0]


def around(axis):
    count = lax.axis_size(axis)
    return [(i, (i + 1) % count) for i in range(count)]


def line_step(up, down, step):
    count = lax.axis_size("fsdp")
    return (
        lax.ppermute(up, "fsdp", [(i, i + 1) for i in range(step - 1, count - 1)]),
        lax.ppermute(down, "fsdp", [(i, i - 1) for i in range(1, count - step + 1)]),
    )


def arrival(up, down, step):
    count, at = lax.axis_size("fsdp"), lax.axis_index("fsdp")
    choices = {}
    owner = 0
    for z in range(count):
        if 2 * z >= count:
            from_up, far = (True, step) if step <= z else (False, step - z)
        else:
            room = count - 1 - z
            from_up, far = (False, step) if step <= room else (True, step - room)
        choices.setdefault((from_up, far), []).append(z)
        owner = jnp.where(at == z, z - far if from_up else z + far, owner)
    pick = None
    for (from_up, far), places in choices.items():
        one = up[far] if from_up else down[far]
        if pick is None:
            pick = one
        else:
            here = functools.reduce(jnp.logical_or, [at == z for z in places])
            pick = jnp.where(here, one, pick)
    return pick, owner


def sum_over_tp(part):
    if lax.axis_size("tp") == 2:
        return part + lax.ppermute(part.astype(BF16), "tp", around("tp")).astype(F32)
    return lax.psum(part.astype(BF16), "tp").astype(F32)


def over_cores(one):
    every = [one]
    for _ in range(1, lax.axis_size("sub")):
        every.append(lax.ppermute(every[-1], "sub", around("sub")))
    return every


def in_range(start, end, at, tokens):
    start, end = start[at : at + 1, :], end[at : at + 1, :]
    position = lax.broadcasted_iota(jnp.int32, (tokens, start.shape[1]), 0)
    return (position >= start) & (position < end)


def low_kernel(sources, count, rank, with_prior, *refs):
    xs, refs = refs[:sources], refs[sources:]
    blocks, (start, end), refs = refs[:count], refs[count : count + 2], refs[count + 2 :]
    prior = refs[0] if with_prior else None
    out, total = refs[-2:]
    tokens = xs[0].shape[0]
    step = pl.program_id(0)
    rows = jnp.concatenate([block[...] for block in blocks], axis=0)
    for at, x in enumerate(xs):
        here = pl.ds(at * tokens, tokens)
        part = lax.dot_general(x[...], rows, TRANS_B, preferred_element_type=F32)

        @pl.when(step == 0)
        def _():
            total[here, :] = part

        @pl.when(step > 0)
        def _():
            total[here, :] += part

        @pl.when(step == pl.num_programs(0) - 1)
        def _():
            chosen = jnp.where(in_range(start, end, at, tokens), total[here, :], 0.0)
            low = chosen[:, :LANES]
            for lane in range(LANES, chosen.shape[1], LANES):
                low = low + chosen[:, lane : lane + LANES]
            turn = LANES // 2
            while turn >= rank:
                low = low + pltpu.roll(low, turn, 1)
                turn //= 2
            out[here, :] = low + prior[here, :] if with_prior else low


def low_rank(xs, blocks, start, end, rank, prior=None):
    tokens, depth = xs[0].shape
    chunk = min(depth, 1024)
    columns = start.shape[1]
    rows = len(xs) * tokens
    fixed = lambda shape: pl.BlockSpec(shape, lambda k: (0, 0))
    operands = [*xs, *blocks, start, end] + ([] if prior is None else [prior])
    in_specs = [pl.BlockSpec((tokens, chunk), lambda k: (0, k)) for _ in xs]
    in_specs += [pl.BlockSpec((b.shape[0], chunk), lambda k: (0, k)) for b in blocks]
    in_specs += [fixed(start.shape), fixed(end.shape)]
    if prior is not None:
        in_specs.append(fixed((rows, LANES)))
    return pl.pallas_call(
        functools.partial(low_kernel, len(xs), len(blocks), rank, prior is not None),
        grid=(depth // chunk,),
        in_specs=in_specs,
        out_specs=fixed((rows, LANES)),
        out_shape=jax.ShapeDtypeStruct((rows, LANES), F32),
        scratch_shapes=[pltpu.VMEM((rows, columns), F32)],
        compiler_params=pltpu.CompilerParams(vmem_limit_bytes=24 * 2**20),
        cost_estimate=SMALL,
    )(*operands)


def spread(low, start, end, at):
    tokens, columns = low.shape[0], start.shape[1]
    repeated = jnp.concatenate([low] * (columns // LANES), axis=1)
    return jnp.where(in_range(start, end, at, tokens), repeated, 0.0).astype(BF16)


def spread_kernel(low, start, end, out):
    out[...] = spread(low[...], start, end, 0)


def spread_out(low, start, end):
    return pl.pallas_call(
        spread_kernel,
        out_shape=jax.ShapeDtypeStruct((low.shape[0], start.shape[1]), BF16),
        compiler_params=pltpu.CompilerParams(vmem_limit_bytes=24 * 2**20),
        cost_estimate=SMALL,
    )(low, start, end)


def outer_kernel(scale, parts, low, start, end, *refs):
    xs, outs, wide = refs[: -1 - parts], refs[-1 - parts : -1], refs[-1]
    tokens = xs[0].shape[0]

    @pl.when(pl.program_id(0) == 0)
    def _():
        for at in range(len(xs)):
            here = pl.ds(at * tokens, tokens)
            wide[here, :] = spread(low[here, :], start, end, at)

    total = None
    for at, x in enumerate(xs):
        part = lax.dot_general(
            wide[pl.ds(at * tokens, tokens), :], x[...], TRANS_A, preferred_element_type=F32
        )
        total = part if total is None else total + part
    if scale != 1.0:
        total = total * scale
    rows = total.shape[0] // parts
    for at, out in enumerate(outs):
        out[...] = total[at * rows : (at + 1) * rows]


def outer(low, start, end, xs, scale, parts):
    tokens, features = xs[0].shape
    columns = start.shape[1]
    rows = columns // parts
    chunk = min(features, 512)
    fixed = lambda shape: pl.BlockSpec(shape, lambda k: (0, 0))
    moving = lambda count: pl.BlockSpec((count, chunk), lambda k: (0, k))
    return pl.pallas_call(
        functools.partial(outer_kernel, scale, parts),
        grid=(features // chunk,),
        in_specs=[fixed(low.shape), fixed(start.shape), fixed(end.shape)] + [moving(tokens)] * len(xs),
        out_specs=[moving(rows)] * parts,
        out_shape=[jax.ShapeDtypeStruct((rows, features), F32)] * parts,
        scratch_shapes=[pltpu.VMEM((len(xs) * tokens, columns), BF16)],
        compiler_params=pltpu.CompilerParams(vmem_limit_bytes=32 * 2**20),
        cost_estimate=SMALL,
    )(low, start, end, *xs)


def input_gradient_kernel(shards, factor_blocks, _, *refs):
    grads, weights = refs[:shards], refs[shards : 2 * shards]
    wide = refs[2 * shards]
    factors = refs[2 * shards + 1 : 2 * shards + 1 + factor_blocks]
    out = refs[-1]
    rows = jnp.concatenate([factor[...] for factor in factors], axis=0)
    total = jnp.dot(wide[...], rows, preferred_element_type=F32)
    for grad, weight in zip(grads, weights, strict=True):
        total += lax.dot_general(grad[...], weight[...], TRANS_B, preferred_element_type=F32)
    out[...] = total.astype(out.dtype)


def input_gradient_part(scalars, copies, grad_full, weights, wide, factors, so_far):
    tokens, features = wide.shape[0], factors[0].shape[1]
    shards = len(weights)
    rows, width = weights[-1].shape[0] if shards > 1 else features // copies, weights[0].shape[1]
    block = min(rows, 512)
    steps = rows // block
    at = lambda j, s: (0, s[shards] * steps + j)
    in_specs = [
        pl.BlockSpec((tokens, width), functools.partial(lambda k, j, s: (0, s[k]), k))
        for k in range(shards)
    ]
    in_specs.append(pl.BlockSpec((block, width), lambda j, s: (s[shards] * steps + j, 0)))
    in_specs += [pl.BlockSpec((block, width), lambda j, s: (j, 0)) for _ in range(shards - 1)]
    in_specs += [pl.BlockSpec(wide.shape, lambda j, s: (0, 0))]
    in_specs += [pl.BlockSpec((factor.shape[0], block), at) for factor in factors]
    operands = [scalars] + [grad_full] * shards + list(weights) + [wide] + list(factors)
    aliases = {}
    if so_far is not None:
        in_specs.append(pl.BlockSpec(memory_space=pl.ANY))
        operands.append(so_far)
        aliases = {len(operands) - 1: 0}
    return pl.pallas_call(
        functools.partial(input_gradient_kernel, shards, len(factors)),
        grid_spec=pltpu.PrefetchScalarGridSpec(
            num_scalar_prefetch=1,
            grid=(steps,),
            in_specs=in_specs,
            out_specs=pl.BlockSpec((tokens, block), at),
        ),
        out_shape=jax.ShapeDtypeStruct((tokens, features), BF16),
        input_output_aliases=aliases,
        compiler_params=pltpu.CompilerParams(vmem_limit_bytes=32 * 2**20),
        cost_estimate=SMALL,
    )(*operands)


def local(activations, output_gradient, base_weight, factor_down, factor_up, counts, owners):
    tokens, features = activations.shape
    columns = output_gradient.shape[1]
    own_slots, rank = factor_down.shape[:2]
    slots = owners.shape[0]
    n, subs, groups = lax.axis_size("fsdp"), lax.axis_size("sub"), lax.axis_size("groups")
    z, sub, y = lax.axis_index("fsdp"), lax.axis_index("sub"), lax.axis_index("groups")
    own_rows = own_slots * rank
    other_core = [(i, (i + 1) % subs) for i in range(subs)]

    both = range(subs)

    up_here = factor_up.reshape(own_rows, columns)
    up_line = [up_here] + [
        lax.ppermute(up_here, "fsdp", [(i, (i + far) % n) for i in range(n)]) for far in range(1, n)
    ]
    factor_here = factor_down.reshape(own_rows, features)
    fd_up, fd_down = [factor_here], [factor_here]
    copies = groups * subs
    part_rows, width = base_weight.shape[0] // copies, base_weight.shape[1]
    weight_here = lax.dynamic_index_in_dim(
        base_weight.reshape(copies, part_rows, width), y * subs + sub, 0, keepdims=False
    )
    w_up, w_down = [weight_here], [weight_here]

    def line_on(ups, downs, step, *earlier):
        if step < n:
            source = [after(one, *earlier) for one in (ups[-1], downs[-1])]
            one, two = line_step(*source, step)
            ups.append(one)
            downs.append(two)

    line_on(fd_up, fd_down, 1)
    x_cores = over_cores(activations)
    g_cores = over_cores(output_gradient)
    count_cores = over_cores(counts[0])
    if lax.axis_size("tp") == 2:
        other = lax.ppermute(output_gradient, "tp", around("tp"))
        first = lax.axis_index("tp") == 0
        grad_full = jnp.concatenate(
            [jnp.where(first, output_gradient, other), jnp.where(first, other, output_gradient)], axis=1
        )
    else:
        grad_full = lax.all_gather(output_gradient, "tp", axis=1, tiled=True)

    hot = owners[:, None] == lax.broadcasted_iota(jnp.int32, (slots, slots), 1)
    bounds = []
    for count in count_cores:
        seg_ends = jnp.cumsum(count)
        starts = jnp.sum(jnp.where(hot, (seg_ends - count)[:, None], 0), axis=0)
        ends = jnp.sum(jnp.where(hot, seg_ends[:, None], 0), axis=0)
        bounds.append((starts, ends))

    def ranges(devices, cores):
        which = jnp.concatenate(
            [(at * subs + core) * own_slots + jnp.arange(own_slots, dtype=jnp.int32) for at, core in devices]
        )
        which = jnp.repeat(which, rank)
        found = which[:, None] == jnp.arange(slots, dtype=jnp.int32)[None, :]
        return tuple(
            jnp.stack([jnp.sum(jnp.where(found, bounds[b][end][None, :], 0), axis=1) for b in cores])
            for end in range(2)
        )

    along_line = ranges([((z - j) % n, sub) for j in range(n)], both)
    round_0 = [*up_line[1:], fd_up[1], fd_down[1], grad_full, *x_cores[1:], *g_cores[1:]]

    line_on(fd_up, fd_down, 2, *round_0)
    line_on(w_up, w_down, 1, *round_0)
    low_back = low_rank([after(g_cores[0], *round_0), *g_cores[1:]], up_line, *along_line, rank)
    low_back = sum_over_tp(adapter_scale_factor * low_back)
    down_blocks = outer(low_back, *along_line, x_cores, 1.0, n)
    whose, factors = [z], [over_cores(after(factor_here, *round_0))]

    def factor_arrives(step):
        mine, owner = arrival(fd_up, fd_down, step)
        whose.append(owner)
        factors.append(over_cores(mine))

    factor_arrives(1)
    round_1 = [fd_up[-1], fd_down[-1], w_up[-1], w_down[-1], *down_blocks, *factors[0], *factors[1]]

    from_above = from_below = None

    def sum_on(step, *earlier):
        lower, upper = down_blocks[n - step], down_blocks[step]
        if step > 1:
            lower, upper = lower + from_above.astype(F32), upper + from_below.astype(F32)
        lower, upper = (after(one.astype(BF16), *earlier) for one in (lower, upper))
        return (
            lax.ppermute(lower, "fsdp", [(i, i - 1) for i in range(n - step, n)]),
            lax.ppermute(upper, "fsdp", [(i, i + 1) for i in range(step)]),
        )

    weight_arrivals = []

    def weight_arrives(step, *earlier):
        mine = [after(arrival(w_up, w_down, step)[0], *earlier)]
        for _ in range(1, groups):
            mine.append(lax.ppermute(mine[-1], "groups", around("groups")))
        weight_arrivals.append(mine)

    for step in range(3, n):
        line_on(fd_up, fd_down, step, *round_1)
    line_on(w_up, w_down, 2, *round_1)
    from_above, from_below = sum_on(1, *round_1)
    weight_arrives(1, *round_1)
    for step in range(2, n - 1):
        factor_arrives(step)
    early = len(factors)
    if early * own_rows % LANES:
        early = 0
    low_in = None
    if early:
        low_in = low_rank(
            [after(x_cores[0], *round_1), *x_cores[1:]],
            [pair[0] for pair in factors[:early]],
            *ranges([(at, sub) for at in whose[:early]], both),
            rank,
        )
    round_2 = [fd_up[-1], fd_down[-1], w_up[-1], w_down[-1], from_above, from_below]
    round_2 += weight_arrivals[0][1:] + factors[-1] + ([] if low_in is None else [low_in])

    for step in range(3, n):
        line_on(w_up, w_down, step, *round_2)
    for step in range(2, n - 1):
        from_above, from_below = sum_on(step, *round_2)
        weight_arrives(step, *round_2)
    for step in range(max(2, n - 1), n):
        factor_arrives(step)
    low_in = low_rank(
        [after(x_cores[0], *round_2), *x_cores[1:]],
        [pair[0] for pair in factors[early:]],
        *ranges([(at, sub) for at in whose[early:]], both),
        rank,
        low_in,
    )
    low_in = sum_over_tp(low_in)
    up_pieces = outer(low_in, *along_line, g_cores, adapter_scale_factor, n)
    low_mine = low_back[:tokens]
    for b in range(1, subs):
        theirs = low_back[b * tokens : (b + 1) * tokens].astype(BF16)
        low_mine = low_mine + lax.ppermute(
            theirs, "sub", [(i, (i - b) % subs) for i in range(subs)]
        ).astype(F32)
    wide = spread_out(low_mine, *ranges([(at, (sub - b) % subs) for at in whose for b in both], [0]))
    round_3 = [w_up[-1], w_down[-1], from_above, from_below, *up_pieces, wide, *factors[-1]]
    round_3 += weight_arrivals[-1][1:]

    if n > 2:
        from_above, from_below = sum_on(n - 1, *round_3)
        weight_arrives(n - 1, *round_3)
    grad_down = down_blocks[0] + from_above.astype(F32) + from_below.astype(F32)
    up_total = up_pieces[0]
    for far in range(1, n):
        got = lax.ppermute(
            after(up_pieces[far].astype(BF16), *round_3), "fsdp", [(i, (i - far) % n) for i in range(n)]
        )
        up_total = up_total + got.astype(F32)
    weight_parts = [[[base_weight] for _ in range(groups)] for _ in both]
    for arrived in weight_arrivals:
        for a, one in enumerate(arrived):
            for b, held in enumerate(over_cores(one)):
                weight_parts[b][a].append(held)
    all_factors = [one for pair in factors for one in pair]
    input_gradient = None
    for a in range(groups):
        for b in both:
            part = ((y - a) % groups) * subs + (sub - b) % subs
            scalars = jnp.stack(whose + [part]).astype(jnp.int32)
            input_gradient = input_gradient_part(
                scalars, copies, grad_full, weight_parts[b][a], wide, all_factors, input_gradient
            )
    return (
        input_gradient,
        grad_down.reshape(own_slots, rank, features),
        up_total.reshape(own_slots, rank, columns),
    )


def solution(mesh):
    placed = (
        P(("groups", "fsdp", "sub"), "tp"),
        P(("groups", "fsdp", "sub"), "tp"),
        P("tp", "fsdp"),
        P(("groups", "fsdp", "sub"), None, "tp"),
        P(("groups", "fsdp", "sub"), None, "tp"),
        P(("groups", "fsdp", "sub"), None),
        P("groups"),
    )
    return jax.shard_map(
        local,
        mesh=mesh,
        in_specs=placed,
        out_specs=(
            P(("groups", "fsdp", "sub"), "tp"),
            P(("groups", "fsdp", "sub"), None, "tp"),
            P(("groups", "fsdp", "sub"), None, "tp"),
        ),
        check_vma=False,
    )
```

```python
import functools

import jax
import jax.numpy as jnp
from jax import lax
from jax.experimental import pallas as pl
from jax.experimental.pallas import tpu as pltpu
from jax.sharding import PartitionSpec as P

adapter_scale_factor = 0.25
F32 = jnp.float32
BF16 = jnp.bfloat16
LANES = 128
PIECES = 1
TRANS_B = (((1,), (1,)), ((), ()))
SMALL = pl.CostEstimate(flops=1, bytes_accessed=1, transcendentals=0)
LONG = pl.CostEstimate(flops=20 * 10**9, bytes_accessed=1, transcendentals=0)
TRANS_A = (((0,), (0,)), ((), ()))


def after(value, *earlier):
    return lax.optimization_barrier((value, *earlier))[0]


def mark_kernel(*refs):
    refs[-1][...] = jnp.zeros_like(refs[-1])


def mark(cost, *arrays):
    return pl.pallas_call(
        mark_kernel,
        in_specs=[pl.BlockSpec(memory_space=pl.ANY) for _ in arrays],
        out_shape=jax.ShapeDtypeStruct((8, LANES), F32),
        compiler_params=pltpu.CompilerParams(vmem_limit_bytes=2**20),
        cost_estimate=cost,
    )(*arrays)


def around(axis):
    count = lax.axis_size(axis)
    return [(i, (i + 1) % count) for i in range(count)]


def line_step(up, down, step):
    count, at = lax.axis_size("fsdp"), lax.axis_index("fsdp")
    if step == count - 1 and count >= 4:
        both = lax.ppermute(
            jnp.where(at == 1, down, up), "fsdp", [(count - 2, count - 1), (1, 0)]
        )
        return both, both
    return (
        lax.ppermute(up, "fsdp", [(i, i + 1) for i in range(step - 1, count - 1)]),
        lax.ppermute(down, "fsdp", [(i, i - 1) for i in range(1, count - step + 1)]),
    )


def arrives(step, place):
    count = lax.axis_size("fsdp")
    if 2 * place >= count:
        return (True, step) if step <= place else (False, step - place)
    room = count - 1 - place
    return (False, step) if step <= room else (True, step - room)


def arrival(up, down, step):
    count, at = lax.axis_size("fsdp"), lax.axis_index("fsdp")
    choices = {}
    for place in range(count):
        choices.setdefault(arrives(step, place), []).append(place)
    pick = None
    for (from_up, far), places in choices.items():
        one = up[far] if from_up else down[far]
        here = functools.reduce(jnp.logical_or, [at == place for place in places])
        pick = one if pick is None else jnp.where(here, one, pick)
    return pick


def arrival_owner(step):
    count, at = lax.axis_size("fsdp"), lax.axis_index("fsdp")
    owner = 0
    for place in range(count):
        from_up, far = arrives(step, place)
        owner = jnp.where(at == place, place - far if from_up else place + far, owner)
    return owner


def sum_over_tp(part):
    if lax.axis_size("tp") == 2:
        return part + lax.ppermute(part.astype(BF16), "tp", around("tp")).astype(F32)
    return lax.psum(part.astype(BF16), "tp").astype(F32)


def over_cores(one):
    every = [one]
    for _ in range(1, lax.axis_size("sub")):
        every.append(lax.ppermute(every[-1], "sub", around("sub")))
    return every


def in_range(start, end, at, tokens):
    start, end = start[at : at + 1, :], end[at : at + 1, :]
    position = lax.broadcasted_iota(jnp.int32, (tokens, start.shape[1]), 0)
    return (position >= start) & (position < end)


def row_pieces(xs, chunk):
    rows = xs[0].shape[0] // PIECES
    one = lambda piece: pl.BlockSpec((rows, chunk), lambda k: (piece, k))
    return [one(piece) for _ in xs for piece in range(PIECES)]


def low_kernel(sources, count, rank, with_prior, *refs):
    xs, refs = refs[: sources * PIECES], refs[sources * PIECES :]
    blocks, (start, end), refs = refs[:count], refs[count : count + 2], refs[count + 2 :]
    prior = refs[0] if with_prior else None
    out, total = refs[-2:]
    piece = xs[0].shape[0]
    tokens = piece * PIECES
    step = pl.program_id(0)
    rows = jnp.concatenate([block[...] for block in blocks], axis=0)
    for at, x in enumerate(xs):
        here = pl.ds(at * piece, piece)
        part = lax.dot_general(x[...], rows, TRANS_B, preferred_element_type=F32)

        @pl.when(step == 0)
        def _():
            total[here, :] = part

        @pl.when(step > 0)
        def _():
            total[here, :] += part

    @pl.when(step == pl.num_programs(0) - 1)
    def _():
        for at in range(sources):
            here = pl.ds(at * tokens, tokens)
            chosen = jnp.where(in_range(start, end, at, tokens), total[here, :], 0.0)
            low = chosen[:, :LANES]
            for lane in range(LANES, chosen.shape[1], LANES):
                low = low + chosen[:, lane : lane + LANES]
            turn = LANES // 2
            while turn >= rank:
                low = low + pltpu.roll(low, turn, 1)
                turn //= 2
            out[here, :] = low + prior[here, :] if with_prior else low


def low_rank(xs, blocks, start, end, rank, prior=None):
    tokens, depth = xs[0].shape
    chunk = min(depth, 1024)
    columns = start.shape[1]
    rows = len(xs) * tokens
    fixed = lambda shape: pl.BlockSpec(shape, lambda k: (0, 0))
    operands = [x for x in xs for _ in range(PIECES)]
    operands += [*blocks, start, end] + ([] if prior is None else [prior])
    in_specs = row_pieces(xs, chunk)
    in_specs += [pl.BlockSpec((b.shape[0], chunk), lambda k: (0, k)) for b in blocks]
    in_specs += [fixed(start.shape), fixed(end.shape)]
    if prior is not None:
        in_specs.append(fixed((rows, LANES)))
    return pl.pallas_call(
        functools.partial(low_kernel, len(xs), len(blocks), rank, prior is not None),
        grid=(depth // chunk,),
        in_specs=in_specs,
        out_specs=fixed((rows, LANES)),
        out_shape=jax.ShapeDtypeStruct((rows, LANES), F32),
        scratch_shapes=[pltpu.VMEM((rows, columns), F32)],
        compiler_params=pltpu.CompilerParams(vmem_limit_bytes=20 * 2**20),
        cost_estimate=SMALL,
    )(*operands)


def spread(low, start, end, at):
    tokens, columns = low.shape[0], start.shape[1]
    repeated = jnp.concatenate([low] * (columns // LANES), axis=1)
    return jnp.where(in_range(start, end, at, tokens), repeated, 0.0).astype(BF16)


def spread_kernel(low, start, end, *outs):
    tokens = outs[0].shape[0]
    for at, out in enumerate(outs):
        out[...] = spread(low[pl.ds(at * tokens, tokens), :], start, end, at)


def spread_out(low, start, end):
    sources, columns = start.shape
    return pl.pallas_call(
        spread_kernel,
        out_shape=[jax.ShapeDtypeStruct((low.shape[0] // sources, columns), BF16)] * sources,
        compiler_params=pltpu.CompilerParams(vmem_limit_bytes=24 * 2**20),
        cost_estimate=SMALL,
    )(low, start, end)


def outer_kernel(scale, parts, low, start, end, *refs):
    xs, outs, wide = refs[: -1 - parts], refs[-1 - parts : -1], refs[-1]
    sources = len(xs) // PIECES
    tokens = low.shape[0] // sources

    @pl.when(pl.program_id(0) == 0)
    def _():
        for at in range(sources):
            here = pl.ds(at * tokens, tokens)
            wide[here, :] = spread(low[here, :], start, end, at)

    every = jnp.concatenate([x[...] for x in xs], axis=0)
    total = lax.dot_general(wide[...], every, TRANS_A, preferred_element_type=F32)
    if scale != 1.0:
        total = total * scale
    rows = total.shape[0] // parts
    for at, out in enumerate(outs):
        out[...] = total[at * rows : (at + 1) * rows].astype(out.dtype)


def outer(low, start, end, xs, scale, parts):
    tokens, features = xs[0].shape
    columns = start.shape[1]
    rows = columns // parts
    chunk = min(features, 512)
    fixed = lambda shape: pl.BlockSpec(shape, lambda k: (0, 0))
    moving = lambda count: pl.BlockSpec((count, chunk), lambda k: (0, k))
    return pl.pallas_call(
        functools.partial(outer_kernel, scale, parts),
        grid=(features // chunk,),
        in_specs=[fixed(low.shape), fixed(start.shape), fixed(end.shape)] + row_pieces(xs, chunk),
        out_specs=[moving(rows)] * parts,
        out_shape=[
            jax.ShapeDtypeStruct((rows, features), F32 if at == 0 else BF16) for at in range(parts)
        ],
        scratch_shapes=[pltpu.VMEM((len(xs) * tokens, columns), BF16)],
        compiler_params=pltpu.CompilerParams(vmem_limit_bytes=20 * 2**20),
        cost_estimate=SMALL,
    )(low, start, end, *[x for x in xs for _ in range(PIECES)])


def trade_kernel(_, *refs):
    *factors, other, low, out = refs
    tokens, at = out.shape[0], factors[0].shape[1]
    rows = factors[0].shape[0]
    for i, factor in enumerate(factors):
        out[i * rows : (i + 1) * rows, :at] = factor[...]
    out[:, at : at + other.shape[1]] = other[...]
    at += other.shape[1]
    for first in range(0, low.shape[0], tokens):
        out[:, at : at + LANES] = low[first : first + tokens, :].astype(BF16)
        at += LANES


def to_trade(place, factors, other, low, half):
    tokens = other.shape[0]
    width = half + other.shape[1] + low.shape[0] // tokens * LANES
    fixed = lambda one: pl.BlockSpec(one.shape, lambda i, s: (0, 0))
    return pl.pallas_call(
        trade_kernel,
        grid_spec=pltpu.PrefetchScalarGridSpec(
            num_scalar_prefetch=1,
            grid=(1,),
            in_specs=[pl.BlockSpec((one.shape[0], half), lambda i, s: (0, s[0])) for one in factors]
            + [fixed(other), fixed(low)],
            out_specs=pl.BlockSpec((tokens, width), lambda i, s: (0, 0)),
        ),
        out_shape=jax.ShapeDtypeStruct((tokens, width), BF16),
        compiler_params=pltpu.CompilerParams(vmem_limit_bytes=24 * 2**20),
        cost_estimate=SMALL,
    )(jnp.asarray(place, jnp.int32).reshape(1), *factors, other, low)


def input_gradient_kernel(sources, shards, factor_blocks, _, *refs):
    weights, refs = refs[:shards], refs[shards:]
    factors, refs = refs[:factor_blocks], refs[factor_blocks:]
    wides, refs = refs[:sources], refs[sources:]
    grads, outs = refs[: sources * shards], refs[-sources:]
    rows = jnp.concatenate([factor[...] for factor in factors], axis=0)
    for at in range(sources):
        total = jnp.dot(wides[at][...], rows, preferred_element_type=F32)
        for grad, weight in zip(grads[at * shards : (at + 1) * shards], weights, strict=True):
            total += lax.dot_general(grad[...], weight[...], TRANS_B, preferred_element_type=F32)
        outs[at][...] = total.astype(BF16)


def input_gradient_part(part, inner, whose, rows, grads, weights, wides, factors, halves, so_far):
    features = factors[0].shape[1]
    sources, shards, tokens = len(grads), len(weights), grads[0].shape[0]
    width = weights[0].shape[1]
    block = min(rows, 512)
    steps = rows // block
    scalars = jnp.stack([*whose, part, inner]).astype(jnp.int32)
    in_specs = [pl.BlockSpec((block, width), lambda j, s: (s[shards] * steps + j, 0))]
    in_specs += [pl.BlockSpec((block, width), lambda j, s: (j, 0)) for _ in range(shards - 1)]
    in_specs += [
        pl.BlockSpec((one.shape[0], block), lambda j, s: (0, s[shards] * steps + j)) for one in factors
    ]
    in_specs += [
        pl.BlockSpec((one.shape[0], block), lambda j, s: (0, s[shards + 1] * steps + j)) for one in halves
    ]
    in_specs += [pl.BlockSpec(wide.shape, lambda j, s: (0, 0)) for wide in wides]
    in_specs += [
        pl.BlockSpec((tokens, width), functools.partial(lambda k, j, s: (0, s[k]), k))
        for _ in grads
        for k in range(shards)
    ]
    operands = [scalars, *weights, *factors, *halves, *wides]
    operands += [grad for grad in grads for _ in range(shards)]
    aliases = {}
    if so_far is not None:
        in_specs.append(pl.BlockSpec(memory_space=pl.ANY))
        operands.append(so_far)
        aliases = {len(operands) - 1: 0}
    return pl.pallas_call(
        functools.partial(input_gradient_kernel, sources, shards, len(factors) + len(halves)),
        grid_spec=pltpu.PrefetchScalarGridSpec(
            num_scalar_prefetch=1,
            grid=(steps,),
            in_specs=in_specs,
            out_specs=[pl.BlockSpec((tokens, block), lambda j, s: (0, s[shards] * steps + j))]
            + [pl.BlockSpec((tokens, block), lambda j, s: (0, j))] * (sources - 1),
        ),
        out_shape=[jax.ShapeDtypeStruct((tokens, features), BF16)]
        + [jax.ShapeDtypeStruct((tokens, rows), BF16)] * (sources - 1),
        input_output_aliases=aliases,
        compiler_params=pltpu.CompilerParams(vmem_limit_bytes=56 * 2**20),
        cost_estimate=SMALL,
    )(*operands)


def local(activations, output_gradient, base_weight, factor_down, factor_up, counts, owners):
    tokens, features = activations.shape
    columns = output_gradient.shape[1]
    own_slots, rank = factor_down.shape[:2]
    slots = owners.shape[0]
    n, subs, groups = lax.axis_size("fsdp"), lax.axis_size("sub"), lax.axis_size("groups")
    z, sub, y = lax.axis_index("fsdp"), lax.axis_index("sub"), lax.axis_index("groups")
    own_rows = own_slots * rank
    other_core = [(i, (i + 1) % subs) for i in range(subs)]

    both = range(subs)
    events = []

    def event(*arrays, cost=SMALL):
        events.append(mark(cost, *arrays, *events[-1:]))
        return events[-1]

    half = features // subs
    copies = groups * subs
    part_rows, width = base_weight.shape[0] // copies, base_weight.shape[1]

    def line_on(ups, downs, step, *earlier):
        if step < n:
            one, two = line_step(after(ups[-1], *earlier), after(downs[-1], *earlier), step)
            ups.append(one)
            downs.append(two)

    g_cores = over_cores(output_gradient)
    count_cores = over_cores(counts[0])
    soon = [*g_cores[1:], *count_cores[1:]]
    x_cores = over_cores(after(activations, *soon))
    factors = [factor_down.reshape(own_rows, features)]

    def factor_on(*earlier):
        if len(factors) < n:
            factors.append(lax.ppermute(after(factors[-1], *earlier), "fsdp", around("fsdp")))

    up_here = factor_up.reshape(own_rows, columns)
    up_line = [up_here] + [
        lax.ppermute(up_here, "fsdp", [(i, (i + far) % n) for i in range(n)]) for far in range(1, n)
    ]
    factor_on(*soon)

    hot = owners[:, None] == lax.broadcasted_iota(jnp.int32, (slots, slots), 1)
    bounds = []
    for count in count_cores:
        seg_ends = jnp.cumsum(count)
        starts = jnp.sum(jnp.where(hot, (seg_ends - count)[:, None], 0), axis=0)
        ends = jnp.sum(jnp.where(hot, seg_ends[:, None], 0), axis=0)
        bounds.append((starts, ends))

    def ranges(devices):
        which = jnp.concatenate(
            [(at * subs + core) * own_slots + jnp.arange(own_slots, dtype=jnp.int32) for at, core in devices]
        )
        which = jnp.repeat(which, rank)
        found = which[:, None] == jnp.arange(slots, dtype=jnp.int32)[None, :]
        return tuple(
            jnp.stack([jnp.sum(jnp.where(found, one[end][None, :], 0), axis=1) for one in bounds])
            for end in range(2)
        )

    along_line = ranges([((z - j) % n, sub) for j in range(n)])
    weight_here = lax.dynamic_index_in_dim(
        base_weight.reshape(copies, part_rows, width), sub * groups + y, 0, keepdims=False
    )
    w_up, w_down = [weight_here], [weight_here]
    came = event(*up_line[1:], weight_here)

    line_on(w_up, w_down, 1, came)
    if lax.axis_size("tp") == 2:
        tp_other = lax.ppermute(after(output_gradient, came), "tp", around("tp"))
        first = lax.axis_index("tp") == 0

        def whole_grad(one, two):
            return jnp.concatenate([jnp.where(first, one, two), jnp.where(first, two, one)], axis=1)
    else:
        tp_other = lax.all_gather(output_gradient, "tp", axis=1, tiled=True)

        def whole_grad(one, two):
            return two

    low_back = low_rank([after(g_cores[0], came), *g_cores[1:]], up_line, *along_line, rank)
    low_back = sum_over_tp(adapter_scale_factor * low_back)
    down_blocks = outer(low_back, *along_line, x_cores, 1.0, n)
    came = event(factors[-1], *x_cores[1:], cost=LONG)
    factor_on(came)
    came = event(w_up[1], w_down[1], tp_other)

    weight_arrivals, whose = [], [z] + [arrival_owner(step) for step in range(1, n)]

    def weight_arrives(step, *earlier):
        mine = [after(arrival(w_up, w_down, step), *earlier)]
        for _ in range(1, groups):
            mine.append(lax.ppermute(mine[-1], "groups", around("groups")))
        weight_arrivals.append(mine)

    def to_sum(step):
        lower, upper = down_blocks[n - step], down_blocks[step]
        if step > 1:
            lower = (lower.astype(F32) + from_above.astype(F32)).astype(BF16)
            upper = (upper.astype(F32) + from_below.astype(F32)).astype(BF16)
        elif n >= 4:
            lower = upper = jnp.where(z == 0, upper, lower)
        return lower, upper

    def sum_on(step, lower, upper, *earlier):
        lower, upper = after(lower, *earlier), after(upper, *earlier)
        if step == 1 and n >= 4:
            got = lax.ppermute(lower, "fsdp", [(n - 1, n - 2), (0, 1)])
            return got, got
        return (
            lax.ppermute(lower, "fsdp", [(i, i - 1) for i in range(n - step, n)]),
            lax.ppermute(upper, "fsdp", [(i, i + 1) for i in range(step)]),
        )

    from_above = from_below = low_in = None
    early = min(n, 3)
    if early * own_rows % LANES:
        early = 0
    for step in range(2, n):
        line_on(w_up, w_down, step, came)
        from_above, from_below = sum_on(step - 1, *to_sum(step - 1), came)
        weight_arrives(step - 1, came)
        if step == n - 1 and early:
            low_in = low_rank(
                [after(x_cores[0], came), *x_cores[1:]],
                factors[:early],
                *ranges([((z - j) % n, sub) for j in range(early)]),
                rank,
            )
        factor_on(event(factors[-1], cost=LONG))
        if step == n - 1:
            low_in = low_rank(
                x_cores, factors[early:], *ranges([((z - j) % n, sub) for j in range(early, n)]), rank, low_in
            )
            low_in = sum_over_tp(low_in)
            came = event(low_in)
        came = event(w_up[-1], w_down[-1], from_above, from_below, *weight_arrivals[-1][1:])

    traded = [None]
    for b in range(1, subs):
        there = to_trade((sub + b) % subs, factors, tp_other, low_back, half)
        there = lax.ppermute(after(there, came), "sub", [(i, (i + b) % subs) for i in range(subs)])
        traded.append((there, there[:, half:]))
    low_back_all, tp_cores = low_back, [tp_other]
    cut = tp_other.shape[1]
    for b in range(1, subs):
        rest = traded[b][1]
        tp_cores.append(rest[:, :cut])
        theirs = [rest[:, cut + at * LANES : cut + (at + 1) * LANES] for at in both]
        theirs = jnp.concatenate([theirs[(at - b) % subs] for at in both], axis=0)
        low_back_all = low_back_all + theirs.astype(F32)
    grads = [whole_grad(one, two) for one, two in zip(g_cores, tp_cores, strict=True)]
    wides = spread_out(
        low_back_all, *ranges([((z - j) % n, (sub - b) % subs) for b in both for j in range(n)])
    )

    up_pieces = outer(low_in, *along_line, g_cores, adapter_scale_factor, n)
    if n > 2:
        lower, upper = to_sum(n - 1)
        lower = jnp.concatenate([lower, up_pieces[1]], axis=1)
        upper = jnp.concatenate([upper, up_pieces[n - 1]], axis=1)

    up_total, round_4 = up_pieces[0], []
    if n > 2:
        from_above, from_below = sum_on(n - 1, lower, upper, came)
        weight_arrives(n - 1, came)
        round_4 += [from_above, from_below]
        up_total = up_total + from_above[:, features:].astype(F32) + from_below[:, features:].astype(F32)
        from_above, from_below = from_above[:, :features], from_below[:, :features]
    for far in range(1, n):
        pairs = [(i, (i - far) % n) for i in range(n)]
        if n > 2 and far == 1:
            far_piece = jnp.where(z == 0, up_pieces[1], up_pieces[n - 1])
            pairs = [(0, n - 1), (n - 1, 0)]
        elif n > 2 and far == n - 1:
            continue
        else:
            far_piece = up_pieces[far]
        got = lax.ppermute(
            after(far_piece, came, *[one[0] for one in traded[1:]]), "fsdp", pairs
        )
        up_total = up_total + got.astype(F32)
        round_4.append(got)
    up_total = up_total + came[0, 0]
    grad_down = down_blocks[0] + from_above.astype(F32) + from_below.astype(F32)
    input_gradient, others = None, []
    for a in range(groups):
        inner = (y - a) % groups
        input_gradient, *for_others = input_gradient_part(
            sub * groups + inner,
            inner,
            whose,
            part_rows,
            grads,
            [base_weight] + [arrived[a] for arrived in weight_arrivals],
            wides,
            factors,
            [one[0] for one in traded[1:]],
            input_gradient,
        )
        others.append(for_others)

    round_4.append(input_gradient)
    for a in range(groups):
        for b, one in enumerate(others[a], 1):
            got = lax.ppermute(
                after(one, *round_4), "sub", [(i, (i - b) % subs) for i in range(subs)]
            )
            part = ((sub + b) % subs) * groups + (y - a) % groups
            input_gradient = lax.dynamic_update_slice_in_dim(input_gradient, got, part * part_rows, axis=1)
    return (
        input_gradient,
        grad_down.reshape(own_slots, rank, features),
        up_total.reshape(own_slots, rank, columns),
    )


def solution(mesh):
    placed = (
        P(("groups", "fsdp", "sub"), "tp"),
        P(("groups", "fsdp", "sub"), "tp"),
        P("tp", "fsdp"),
        P(("groups", "fsdp", "sub"), None, "tp"),
        P(("groups", "fsdp", "sub"), None, "tp"),
        P(("groups", "fsdp", "sub"), None),
        P("groups"),
    )
    return jax.shard_map(
        local,
        mesh=mesh,
        in_specs=placed,
        out_specs=(
            P(("groups", "fsdp", "sub"), "tp"),
            P(("groups", "fsdp", "sub"), None, "tp"),
            P(("groups", "fsdp", "sub"), None, "tp"),
        ),
        check_vma=False,
    )
```

```python
import functools

import jax
import jax.numpy as jnp
from jax import lax
from jax.experimental import pallas as pl
from jax.experimental.pallas import tpu as pltpu
from jax.sharding import PartitionSpec as P

adapter_scale_factor = 0.25
F32 = jnp.float32
BF16 = jnp.bfloat16
LANES = 128
PIECES = 1
TRANS_B = (((1,), (1,)), ((), ()))
SMALL = pl.CostEstimate(flops=1, bytes_accessed=1, transcendentals=0)
LONG = pl.CostEstimate(flops=20 * 10**9, bytes_accessed=1, transcendentals=0)
TRANS_A = (((0,), (0,)), ((), ()))


def after(value, *earlier):
    return lax.optimization_barrier((value, *earlier))[0]


def mark_kernel(*refs):
    refs[-1][...] = jnp.zeros_like(refs[-1])


def mark(cost, *arrays):
    return pl.pallas_call(
        mark_kernel,
        in_specs=[pl.BlockSpec(memory_space=pl.ANY) for _ in arrays],
        out_shape=jax.ShapeDtypeStruct((8, LANES), F32),
        compiler_params=pltpu.CompilerParams(vmem_limit_bytes=2**20),
        cost_estimate=cost,
    )(*arrays)


def around(axis):
    count = lax.axis_size(axis)
    return [(i, (i + 1) % count) for i in range(count)]


def line_step(up, down, step):
    count, at = lax.axis_size("fsdp"), lax.axis_index("fsdp")
    if step == count - 1 and count >= 4:
        both = lax.ppermute(
            jnp.where(at == 1, down, up), "fsdp", [(count - 2, count - 1), (1, 0)]
        )
        return both, both
    return (
        lax.ppermute(up, "fsdp", [(i, i + 1) for i in range(step - 1, count - 1)]),
        lax.ppermute(down, "fsdp", [(i, i - 1) for i in range(1, count - step + 1)]),
    )


def arrives(step, place):
    count = lax.axis_size("fsdp")
    if 2 * place >= count:
        return (True, step) if step <= place else (False, step - place)
    room = count - 1 - place
    return (False, step) if step <= room else (True, step - room)


def arrival(up, down, step):
    count, at = lax.axis_size("fsdp"), lax.axis_index("fsdp")
    choices = {}
    for place in range(count):
        choices.setdefault(arrives(step, place), []).append(place)
    pick = None
    for (from_up, far), places in choices.items():
        one = up[far] if from_up else down[far]
        here = functools.reduce(jnp.logical_or, [at == place for place in places])
        pick = one if pick is None else jnp.where(here, one, pick)
    return pick


def arrival_owner(step):
    count, at = lax.axis_size("fsdp"), lax.axis_index("fsdp")
    owner = 0
    for place in range(count):
        from_up, far = arrives(step, place)
        owner = jnp.where(at == place, place - far if from_up else place + far, owner)
    return owner


def sum_over_tp(part):
    if lax.axis_size("tp") == 2:
        return part + lax.ppermute(part.astype(BF16), "tp", around("tp")).astype(F32)
    return lax.psum(part.astype(BF16), "tp").astype(F32)


def over_cores(one):
    every = [one]
    for _ in range(1, lax.axis_size("sub")):
        every.append(lax.ppermute(every[-1], "sub", around("sub")))
    return every


def in_range(start, end, at, tokens):
    start, end = start[at : at + 1, :], end[at : at + 1, :]
    position = lax.broadcasted_iota(jnp.int32, (tokens, start.shape[1]), 0)
    return (position >= start) & (position < end)


def row_pieces(xs, chunk):
    rows = xs[0].shape[0] // PIECES
    one = lambda piece: pl.BlockSpec((rows, chunk), lambda k: (piece, k))
    return [one(piece) for _ in xs for piece in range(PIECES)]


def low_kernel(sources, count, rank, with_prior, *refs):
    xs, refs = refs[: sources * PIECES], refs[sources * PIECES :]
    blocks, (start, end), refs = refs[:count], refs[count : count + 2], refs[count + 2 :]
    prior = refs[0] if with_prior else None
    out, total = refs[-2:]
    piece = xs[0].shape[0]
    tokens = piece * PIECES
    step = pl.program_id(0)
    rows = jnp.concatenate([block[...] for block in blocks], axis=0)
    for at, x in enumerate(xs):
        here = pl.ds(at * piece, piece)
        part = lax.dot_general(x[...], rows, TRANS_B, preferred_element_type=F32)

        @pl.when(step == 0)
        def _():
            total[here, :] = part

        @pl.when(step > 0)
        def _():
            total[here, :] += part

    @pl.when(step == pl.num_programs(0) - 1)
    def _():
        for at in range(sources):
            here = pl.ds(at * tokens, tokens)
            chosen = jnp.where(in_range(start, end, at, tokens), total[here, :], 0.0)
            low = chosen[:, :LANES]
            for lane in range(LANES, chosen.shape[1], LANES):
                low = low + chosen[:, lane : lane + LANES]
            turn = LANES // 2
            while turn >= rank:
                low = low + pltpu.roll(low, turn, 1)
                turn //= 2
            out[here, :] = low + prior[here, :] if with_prior else low


def low_rank(xs, blocks, start, end, rank, prior=None):
    tokens, depth = xs[0].shape
    chunk = min(depth, 1024)
    columns = start.shape[1]
    rows = len(xs) * tokens
    fixed = lambda shape: pl.BlockSpec(shape, lambda k: (0, 0))
    operands = [x for x in xs for _ in range(PIECES)]
    operands += [*blocks, start, end] + ([] if prior is None else [prior])
    in_specs = row_pieces(xs, chunk)
    in_specs += [pl.BlockSpec((b.shape[0], chunk), lambda k: (0, k)) for b in blocks]
    in_specs += [fixed(start.shape), fixed(end.shape)]
    if prior is not None:
        in_specs.append(fixed((rows, LANES)))
    return pl.pallas_call(
        functools.partial(low_kernel, len(xs), len(blocks), rank, prior is not None),
        grid=(depth // chunk,),
        in_specs=in_specs,
        out_specs=fixed((rows, LANES)),
        out_shape=jax.ShapeDtypeStruct((rows, LANES), F32),
        scratch_shapes=[pltpu.VMEM((rows, columns), F32)],
        compiler_params=pltpu.CompilerParams(vmem_limit_bytes=20 * 2**20),
        cost_estimate=SMALL,
    )(*operands)


def spread(low, start, end, at):
    tokens, columns = low.shape[0], start.shape[1]
    repeated = jnp.concatenate([low] * (columns // LANES), axis=1)
    return jnp.where(in_range(start, end, at, tokens), repeated, 0.0).astype(BF16)


def spread_kernel(low, start, end, *outs):
    tokens = outs[0].shape[0]
    for at, out in enumerate(outs):
        out[...] = spread(low[pl.ds(at * tokens, tokens), :], start, end, at)


def spread_out(low, start, end):
    sources, columns = start.shape
    return pl.pallas_call(
        spread_kernel,
        out_shape=[jax.ShapeDtypeStruct((low.shape[0] // sources, columns), BF16)] * sources,
        compiler_params=pltpu.CompilerParams(vmem_limit_bytes=24 * 2**20),
        cost_estimate=SMALL,
    )(low, start, end)


def outer_kernel(scale, parts, low, start, end, *refs):
    xs, outs, wide = refs[: -1 - parts], refs[-1 - parts : -1], refs[-1]
    sources = len(xs) // PIECES
    tokens = low.shape[0] // sources

    @pl.when(pl.program_id(0) == 0)
    def _():
        for at in range(sources):
            here = pl.ds(at * tokens, tokens)
            wide[here, :] = spread(low[here, :], start, end, at)

    every = jnp.concatenate([x[...] for x in xs], axis=0)
    total = lax.dot_general(wide[...], every, TRANS_A, preferred_element_type=F32)
    if scale != 1.0:
        total = total * scale
    rows = total.shape[0] // parts
    for at, out in enumerate(outs):
        out[...] = total[at * rows : (at + 1) * rows].astype(out.dtype)


def outer(low, start, end, xs, scale, parts):
    tokens, features = xs[0].shape
    columns = start.shape[1]
    rows = columns // parts
    chunk = min(features, 512)
    fixed = lambda shape: pl.BlockSpec(shape, lambda k: (0, 0))
    moving = lambda count: pl.BlockSpec((count, chunk), lambda k: (0, k))
    return pl.pallas_call(
        functools.partial(outer_kernel, scale, parts),
        grid=(features // chunk,),
        in_specs=[fixed(low.shape), fixed(start.shape), fixed(end.shape)] + row_pieces(xs, chunk),
        out_specs=[moving(rows)] * parts,
        out_shape=[
            jax.ShapeDtypeStruct((rows, features), F32 if at == 0 else BF16) for at in range(parts)
        ],
        scratch_shapes=[pltpu.VMEM((len(xs) * tokens, columns), BF16)],
        compiler_params=pltpu.CompilerParams(vmem_limit_bytes=20 * 2**20),
        cost_estimate=SMALL,
    )(low, start, end, *[x for x in xs for _ in range(PIECES)])


def trade_kernel(_, *refs):
    *factors, other, low, out = refs
    tokens, at = out.shape[0], factors[0].shape[1]
    rows = factors[0].shape[0]
    for i, factor in enumerate(factors):
        out[i * rows : (i + 1) * rows, :at] = factor[...]
    out[:, at : at + other.shape[1]] = other[...]
    at += other.shape[1]
    for first in range(0, low.shape[0], tokens):
        out[:, at : at + LANES] = low[first : first + tokens, :].astype(BF16)
        at += LANES


def to_trade(place, factors, other, low, half):
    tokens = other.shape[0]
    width = half + other.shape[1] + low.shape[0] // tokens * LANES
    fixed = lambda one: pl.BlockSpec(one.shape, lambda i, s: (0, 0))
    return pl.pallas_call(
        trade_kernel,
        grid_spec=pltpu.PrefetchScalarGridSpec(
            num_scalar_prefetch=1,
            grid=(1,),
            in_specs=[pl.BlockSpec((one.shape[0], half), lambda i, s: (0, s[0])) for one in factors]
            + [fixed(other), fixed(low)],
            out_specs=pl.BlockSpec((tokens, width), lambda i, s: (0, 0)),
        ),
        out_shape=jax.ShapeDtypeStruct((tokens, width), BF16),
        compiler_params=pltpu.CompilerParams(vmem_limit_bytes=24 * 2**20),
        cost_estimate=SMALL,
    )(jnp.asarray(place, jnp.int32).reshape(1), *factors, other, low)


def input_gradient_kernel(sources, shards, factor_blocks, _, *refs):
    weights, refs = refs[:shards], refs[shards:]
    factors, refs = refs[:factor_blocks], refs[factor_blocks:]
    wides, refs = refs[:sources], refs[sources:]
    grads, outs = refs[: sources * shards], refs[-sources:]
    rows = jnp.concatenate([factor[...] for factor in factors], axis=0)
    for at in range(sources):
        total = jnp.dot(wides[at][...], rows, preferred_element_type=F32)
        for grad, weight in zip(grads[at * shards : (at + 1) * shards], weights, strict=True):
            total += lax.dot_general(grad[...], weight[...], TRANS_B, preferred_element_type=F32)
        outs[at][...] = total.astype(BF16)


def input_gradient_part(part, inner, whose, rows, grads, weights, wides, factors, halves, so_far):
    features = factors[0].shape[1]
    sources, shards, tokens = len(grads), len(weights), grads[0].shape[0]
    width = weights[0].shape[1]
    block = min(rows, 512)
    steps = rows // block
    scalars = jnp.stack([*whose, part, inner]).astype(jnp.int32)
    in_specs = [pl.BlockSpec((block, width), lambda j, s: (s[shards] * steps + j, 0))]
    in_specs += [pl.BlockSpec((block, width), lambda j, s: (j, 0)) for _ in range(shards - 1)]
    in_specs += [
        pl.BlockSpec((one.shape[0], block), lambda j, s: (0, s[shards] * steps + j)) for one in factors
    ]
    in_specs += [
        pl.BlockSpec((one.shape[0], block), lambda j, s: (0, s[shards + 1] * steps + j)) for one in halves
    ]
    in_specs += [pl.BlockSpec(wide.shape, lambda j, s: (0, 0)) for wide in wides]
    in_specs += [
        pl.BlockSpec((tokens, width), functools.partial(lambda k, j, s: (0, s[k]), k))
        for _ in grads
        for k in range(shards)
    ]
    operands = [scalars, *weights, *factors, *halves, *wides]
    operands += [grad for grad in grads for _ in range(shards)]
    aliases = {}
    if so_far is not None:
        in_specs.append(pl.BlockSpec(memory_space=pl.ANY))
        operands.append(so_far)
        aliases = {len(operands) - 1: 0}
    return pl.pallas_call(
        functools.partial(input_gradient_kernel, sources, shards, len(factors) + len(halves)),
        grid_spec=pltpu.PrefetchScalarGridSpec(
            num_scalar_prefetch=1,
            grid=(steps,),
            in_specs=in_specs,
            out_specs=[pl.BlockSpec((tokens, block), lambda j, s: (0, s[shards] * steps + j))]
            + [pl.BlockSpec((tokens, block), lambda j, s: (0, j))] * (sources - 1),
        ),
        out_shape=[jax.ShapeDtypeStruct((tokens, features), BF16)]
        + [jax.ShapeDtypeStruct((tokens, rows), BF16)] * (sources - 1),
        input_output_aliases=aliases,
        compiler_params=pltpu.CompilerParams(vmem_limit_bytes=56 * 2**20),
        cost_estimate=SMALL,
    )(*operands)


def local(activations, output_gradient, base_weight, factor_down, factor_up, counts, owners):
    tokens, features = activations.shape
    columns = output_gradient.shape[1]
    own_slots, rank = factor_down.shape[:2]
    slots = owners.shape[0]
    n, subs, groups = lax.axis_size("fsdp"), lax.axis_size("sub"), lax.axis_size("groups")
    z, sub, y = lax.axis_index("fsdp"), lax.axis_index("sub"), lax.axis_index("groups")
    own_rows = own_slots * rank
    other_core = [(i, (i + 1) % subs) for i in range(subs)]

    both = range(subs)
    events = []

    def event(*arrays, cost=SMALL):
        events.append(mark(cost, *arrays, *events[-1:]))
        return events[-1]

    half = features // subs
    copies = groups * subs
    part_rows, width = base_weight.shape[0] // copies, base_weight.shape[1]

    def line_on(ups, downs, step, *earlier):
        if step < n:
            one, two = line_step(after(ups[-1], *earlier), after(downs[-1], *earlier), step)
            ups.append(one)
            downs.append(two)

    g_cores = over_cores(output_gradient)
    count_cores = over_cores(counts[0])
    x_cores = over_cores(activations)
    factors = [factor_down.reshape(own_rows, features)]

    def factor_on(*earlier):
        if len(factors) < n:
            factors.append(lax.ppermute(after(factors[-1], *earlier), "fsdp", around("fsdp")))

    up_here = factor_up.reshape(own_rows, columns)
    up_line = [up_here] + [
        lax.ppermute(up_here, "fsdp", [(i, (i + far) % n) for i in range(n)]) for far in range(1, n)
    ]

    if lax.axis_size("tp") == 2:
        tp_other = lax.ppermute(output_gradient, "tp", around("tp"))
        first = lax.axis_index("tp") == 0

        def whole_grad(one, two):
            return jnp.concatenate([jnp.where(first, one, two), jnp.where(first, two, one)], axis=1)
    else:
        tp_other = lax.all_gather(output_gradient, "tp", axis=1, tiled=True)

        def whole_grad(one, two):
            return two

    hot = owners[:, None] == lax.broadcasted_iota(jnp.int32, (slots, slots), 1)
    bounds = []
    for count in count_cores:
        seg_ends = jnp.cumsum(count)
        starts = jnp.sum(jnp.where(hot, (seg_ends - count)[:, None], 0), axis=0)
        ends = jnp.sum(jnp.where(hot, seg_ends[:, None], 0), axis=0)
        bounds.append((starts, ends))

    def ranges(devices):
        which = jnp.concatenate(
            [(at * subs + core) * own_slots + jnp.arange(own_slots, dtype=jnp.int32) for at, core in devices]
        )
        which = jnp.repeat(which, rank)
        found = which[:, None] == jnp.arange(slots, dtype=jnp.int32)[None, :]
        return tuple(
            jnp.stack([jnp.sum(jnp.where(found, one[end][None, :], 0), axis=1) for one in bounds])
            for end in range(2)
        )

    along_line = ranges([((z - j) % n, sub) for j in range(n)])
    weight_here = lax.dynamic_index_in_dim(
        base_weight.reshape(copies, part_rows, width), sub * groups + y, 0, keepdims=False
    )
    w_up, w_down = [weight_here], [weight_here]
    came = event(*up_line[1:], *g_cores[1:], *x_cores[1:], *along_line, weight_here, tp_other)

    line_on(w_up, w_down, 1, came)
    factor_on(came)
    low_back = low_rank([after(g_cores[0], came), *g_cores[1:]], up_line, *along_line, rank)
    low_back = sum_over_tp(adapter_scale_factor * low_back)
    down_blocks = outer(low_back, *along_line, x_cores, 1.0, n)
    came = event(factors[-1], cost=LONG)
    factor_on(came)
    came = event(w_up[1], w_down[1])

    weight_arrivals, whose = [], [z] + [arrival_owner(step) for step in range(1, n)]

    def weight_arrives(step, *earlier):
        mine = [after(arrival(w_up, w_down, step), *earlier)]
        for _ in range(1, groups):
            mine.append(lax.ppermute(mine[-1], "groups", around("groups")))
        weight_arrivals.append(mine)

    def to_sum(step):
        lower, upper = down_blocks[n - step], down_blocks[step]
        if step > 1:
            lower = (lower.astype(F32) + from_above.astype(F32)).astype(BF16)
            upper = (upper.astype(F32) + from_below.astype(F32)).astype(BF16)
        elif n >= 4:
            lower = upper = jnp.where(z == 0, upper, lower)
        return lower, upper

    def sum_on(step, lower, upper, *earlier):
        lower, upper = after(lower, *earlier), after(upper, *earlier)
        if step == 1 and n >= 4:
            got = lax.ppermute(lower, "fsdp", [(n - 1, n - 2), (0, 1)])
            return got, got
        return (
            lax.ppermute(lower, "fsdp", [(i, i - 1) for i in range(n - step, n)]),
            lax.ppermute(upper, "fsdp", [(i, i + 1) for i in range(step)]),
        )

    from_above = from_below = low_in = None
    early = min(n, 3)
    if early * own_rows % LANES:
        early = 0
    for step in range(2, n):
        line_on(w_up, w_down, step, came)
        from_above, from_below = sum_on(step - 1, *to_sum(step - 1), came)
        weight_arrives(step - 1, came)
        if step == n - 1 and early:
            low_in = low_rank(
                [after(x_cores[0], came), *x_cores[1:]],
                factors[:early],
                *ranges([((z - j) % n, sub) for j in range(early)]),
                rank,
            )
        factor_on(event(factors[-1], cost=LONG))
        if step == n - 1:
            low_in = low_rank(
                x_cores, factors[early:], *ranges([((z - j) % n, sub) for j in range(early, n)]), rank, low_in
            )
            low_in = sum_over_tp(low_in)
            came = event(low_in)
        came = event(w_up[-1], w_down[-1], from_above, from_below, *weight_arrivals[-1][1:])

    traded = [None]
    for b in range(1, subs):
        there = to_trade((sub + b) % subs, factors, tp_other, low_back, half)
        there = lax.ppermute(after(there, came), "sub", [(i, (i + b) % subs) for i in range(subs)])
        traded.append((there, there[:, half:]))
    low_back_all, tp_cores = low_back, [tp_other]
    cut = tp_other.shape[1]
    for b in range(1, subs):
        rest = traded[b][1]
        tp_cores.append(rest[:, :cut])
        theirs = [rest[:, cut + at * LANES : cut + (at + 1) * LANES] for at in both]
        theirs = jnp.concatenate([theirs[(at - b) % subs] for at in both], axis=0)
        low_back_all = low_back_all + theirs.astype(F32)
    grads = [whole_grad(one, two) for one, two in zip(g_cores, tp_cores, strict=True)]
    wides = spread_out(
        low_back_all + came[:1], *ranges([((z - j) % n, (sub - b) % subs) for b in both for j in range(n)])
    )

    def ig(a, so_far, others):
        inner = (y - a) % groups
        so_far, *for_others = input_gradient_part(
            sub * groups + inner,
            inner,
            whose,
            part_rows,
            grads,
            [base_weight] + [arrived[a] for arrived in weight_arrivals],
            wides,
            factors,
            [one[0] for one in traded[1:]],
            so_far,
        )
        return so_far, [*others, for_others]

    if n > 2:
        from_above, from_below = sum_on(n - 1, *to_sum(n - 1), came)
        weight_arrives(n - 1, came)
    grad_down = down_blocks[0] + from_above.astype(F32) + from_below.astype(F32)

    bits = n.bit_length() - 1
    turned = [sum(((place >> k) & 1) << (bits - 1 - k) for k in range(bits)) for place in range(n)]
    up_total, there = outer(
        low_in, *ranges([(z ^ place, sub) for place in turned]), g_cores, adapter_scale_factor, 2
    )
    input_gradient, others, last = None, [], [came]
    for bit in range(bits):
        if bit:
            there = up_total[up_total.shape[0] // 2 :].astype(BF16)
            up_total = up_total[: up_total.shape[0] // 2]
        if bit == 1:
            last += [from_above, from_below, *weight_arrivals[-1][1:]]
        got = lax.ppermute(after(there, *last), "fsdp", [(i, i ^ (1 << bit)) for i in range(n)])
        up_total = up_total + got.astype(F32)
        if not bit:
            input_gradient, others = ig(0, None, others)
            last = [came, input_gradient]
    for a in range(1, groups):
        input_gradient, others = ig(a, input_gradient, others)

    round_4 = [from_above, from_below, got, input_gradient]
    for a in range(groups):
        for b, one in enumerate(others[a], 1):
            got = lax.ppermute(
                after(one, *round_4), "sub", [(i, (i - b) % subs) for i in range(subs)]
            )
            part = ((sub + b) % subs) * groups + (y - a) % groups
            input_gradient = lax.dynamic_update_slice_in_dim(input_gradient, got, part * part_rows, axis=1)
    return (
        input_gradient,
        grad_down.reshape(own_slots, rank, features),
        up_total.reshape(own_slots, rank, columns),
    )


def solution(mesh):
    placed = (
        P(("groups", "fsdp", "sub"), "tp"),
        P(("groups", "fsdp", "sub"), "tp"),
        P("tp", "fsdp"),
        P(("groups", "fsdp", "sub"), None, "tp"),
        P(("groups", "fsdp", "sub"), None, "tp"),
        P(("groups", "fsdp", "sub"), None),
        P("groups"),
    )
    return jax.shard_map(
        local,
        mesh=mesh,
        in_specs=placed,
        out_specs=(
            P(("groups", "fsdp", "sub"), "tp"),
            P(("groups", "fsdp", "sub"), None, "tp"),
            P(("groups", "fsdp", "sub"), None, "tp"),
        ),
        check_vma=False,
    )
```

```python
import functools

import jax
import jax.numpy as jnp
from jax import lax
from jax.experimental import pallas as pl
from jax.experimental.pallas import tpu as pltpu
from jax.sharding import PartitionSpec as P

adapter_scale_factor = 0.25
F32 = jnp.float32
BF16 = jnp.bfloat16
LANES = 128
PIECES = 1
TRANS_B = (((1,), (1,)), ((), ()))
SMALL = pl.CostEstimate(flops=1, bytes_accessed=1, transcendentals=0)
LONG = pl.CostEstimate(flops=20 * 10**9, bytes_accessed=1, transcendentals=0)
TRANS_A = (((0,), (0,)), ((), ()))


def after(value, *earlier):
    return lax.optimization_barrier((value, *earlier))[0]


def mark_kernel(*refs):
    refs[-1][...] = jnp.zeros_like(refs[-1])


def mark(cost, *arrays):
    return pl.pallas_call(
        mark_kernel,
        in_specs=[pl.BlockSpec(memory_space=pl.ANY) for _ in arrays],
        out_shape=jax.ShapeDtypeStruct((8, LANES), F32),
        compiler_params=pltpu.CompilerParams(vmem_limit_bytes=2**20),
        cost_estimate=cost,
    )(*arrays)


def around(axis):
    count = lax.axis_size(axis)
    return [(i, (i + 1) % count) for i in range(count)]


def line_step(up, down, step):
    count, at = lax.axis_size("fsdp"), lax.axis_index("fsdp")
    if step == count - 1 and count >= 4:
        both = lax.ppermute(
            jnp.where(at == 1, down, up), "fsdp", [(count - 2, count - 1), (1, 0)]
        )
        return both, both
    return (
        lax.ppermute(up, "fsdp", [(i, i + 1) for i in range(step - 1, count - 1)]),
        lax.ppermute(down, "fsdp", [(i, i - 1) for i in range(1, count - step + 1)]),
    )


def arrives(step, place):
    count = lax.axis_size("fsdp")
    if 2 * place >= count:
        return (True, step) if step <= place else (False, step - place)
    room = count - 1 - place
    return (False, step) if step <= room else (True, step - room)


def arrival(up, down, step):
    count, at = lax.axis_size("fsdp"), lax.axis_index("fsdp")
    choices = {}
    for place in range(count):
        choices.setdefault(arrives(step, place), []).append(place)
    pick = None
    for (from_up, far), places in choices.items():
        one = up[far] if from_up else down[far]
        here = functools.reduce(jnp.logical_or, [at == place for place in places])
        pick = one if pick is None else jnp.where(here, one, pick)
    return pick


def arrival_owner(step):
    count, at = lax.axis_size("fsdp"), lax.axis_index("fsdp")
    owner = 0
    for place in range(count):
        from_up, far = arrives(step, place)
        owner = jnp.where(at == place, place - far if from_up else place + far, owner)
    return owner


def sum_over_tp(part):
    if lax.axis_size("tp") == 2:
        return part + lax.ppermute(part.astype(BF16), "tp", around("tp")).astype(F32)
    return lax.psum(part.astype(BF16), "tp").astype(F32)


def over_cores(one):
    every = [one]
    for _ in range(1, lax.axis_size("sub")):
        every.append(lax.ppermute(every[-1], "sub", around("sub")))
    return every


def in_range(start, end, at, tokens):
    start, end = start[at : at + 1, :], end[at : at + 1, :]
    position = lax.broadcasted_iota(jnp.int32, (tokens, start.shape[1]), 0)
    return (position >= start) & (position < end)


def row_pieces(xs, chunk):
    rows = xs[0].shape[0] // PIECES
    one = lambda piece: pl.BlockSpec((rows, chunk), lambda k: (piece, k))
    return [one(piece) for _ in xs for piece in range(PIECES)]


def low_kernel(sources, count, rank, with_prior, *refs):
    xs, refs = refs[: sources * PIECES], refs[sources * PIECES :]
    blocks, (start, end), refs = refs[:count], refs[count : count + 2], refs[count + 2 :]
    prior = refs[0] if with_prior else None
    out, total = refs[-2:]
    piece = xs[0].shape[0]
    tokens = piece * PIECES
    step = pl.program_id(0)
    rows = jnp.concatenate([block[...] for block in blocks], axis=0)
    for at, x in enumerate(xs):
        here = pl.ds(at * piece, piece)
        part = lax.dot_general(x[...], rows, TRANS_B, preferred_element_type=F32)

        @pl.when(step == 0)
        def _():
            total[here, :] = part

        @pl.when(step > 0)
        def _():
            total[here, :] += part

    @pl.when(step == pl.num_programs(0) - 1)
    def _():
        for at in range(sources):
            here = pl.ds(at * tokens, tokens)
            chosen = jnp.where(in_range(start, end, at, tokens), total[here, :], 0.0)
            low = chosen[:, :LANES]
            for lane in range(LANES, chosen.shape[1], LANES):
                low = low + chosen[:, lane : lane + LANES]
            turn = LANES // 2
            while turn >= rank:
                low = low + pltpu.roll(low, turn, 1)
                turn //= 2
            out[here, :] = low + prior[here, :] if with_prior else low


def low_rank(xs, blocks, start, end, rank, prior=None):
    tokens, depth = xs[0].shape
    chunk = min(depth, 1024)
    columns = start.shape[1]
    rows = len(xs) * tokens
    fixed = lambda shape: pl.BlockSpec(shape, lambda k: (0, 0))
    operands = [x for x in xs for _ in range(PIECES)]
    operands += [*blocks, start, end] + ([] if prior is None else [prior])
    in_specs = row_pieces(xs, chunk)
    in_specs += [pl.BlockSpec((b.shape[0], chunk), lambda k: (0, k)) for b in blocks]
    in_specs += [fixed(start.shape), fixed(end.shape)]
    if prior is not None:
        in_specs.append(fixed((rows, LANES)))
    return pl.pallas_call(
        functools.partial(low_kernel, len(xs), len(blocks), rank, prior is not None),
        grid=(depth // chunk,),
        in_specs=in_specs,
        out_specs=fixed((rows, LANES)),
        out_shape=jax.ShapeDtypeStruct((rows, LANES), F32),
        scratch_shapes=[pltpu.VMEM((rows, columns), F32)],
        compiler_params=pltpu.CompilerParams(vmem_limit_bytes=20 * 2**20),
        cost_estimate=SMALL,
    )(*operands)


def spread(low, start, end, at):
    tokens, columns = low.shape[0], start.shape[1]
    repeated = jnp.concatenate([low] * (columns // LANES), axis=1)
    return jnp.where(in_range(start, end, at, tokens), repeated, 0.0).astype(BF16)


def spread_kernel(low, start, end, *outs):
    tokens = outs[0].shape[0]
    for at, out in enumerate(outs):
        out[...] = spread(low[pl.ds(at * tokens, tokens), :], start, end, at)


def spread_out(low, start, end):
    sources, columns = start.shape
    return pl.pallas_call(
        spread_kernel,
        out_shape=[jax.ShapeDtypeStruct((low.shape[0] // sources, columns), BF16)] * sources,
        compiler_params=pltpu.CompilerParams(vmem_limit_bytes=24 * 2**20),
        cost_estimate=SMALL,
    )(low, start, end)


def outer_kernel(scale, parts, low, start, end, *refs):
    xs, outs, wide = refs[: -1 - parts], refs[-1 - parts : -1], refs[-1]
    sources = len(xs) // PIECES
    tokens = low.shape[0] // sources

    @pl.when(pl.program_id(0) == 0)
    def _():
        for at in range(sources):
            here = pl.ds(at * tokens, tokens)
            wide[here, :] = spread(low[here, :], start, end, at)

    every = jnp.concatenate([x[...] for x in xs], axis=0)
    total = lax.dot_general(wide[...], every, TRANS_A, preferred_element_type=F32)
    if scale != 1.0:
        total = total * scale
    rows = total.shape[0] // parts
    for at, out in enumerate(outs):
        out[...] = total[at * rows : (at + 1) * rows].astype(out.dtype)


def outer(low, start, end, xs, scale, parts):
    tokens, features = xs[0].shape
    columns = start.shape[1]
    rows = columns // parts
    chunk = min(features, 512)
    fixed = lambda shape: pl.BlockSpec(shape, lambda k: (0, 0))
    moving = lambda count: pl.BlockSpec((count, chunk), lambda k: (0, k))
    return pl.pallas_call(
        functools.partial(outer_kernel, scale, parts),
        grid=(features // chunk,),
        in_specs=[fixed(low.shape), fixed(start.shape), fixed(end.shape)] + row_pieces(xs, chunk),
        out_specs=[moving(rows)] * parts,
        out_shape=[
            jax.ShapeDtypeStruct((rows, features), F32 if at == 0 else BF16) for at in range(parts)
        ],
        scratch_shapes=[pltpu.VMEM((len(xs) * tokens, columns), BF16)],
        compiler_params=pltpu.CompilerParams(vmem_limit_bytes=20 * 2**20),
        cost_estimate=SMALL,
    )(low, start, end, *[x for x in xs for _ in range(PIECES)])


def trade_kernel(_, *refs):
    *factors, other, low, out = refs
    tokens, at = out.shape[0], factors[0].shape[1]
    rows = factors[0].shape[0]
    for i, factor in enumerate(factors):
        out[i * rows : (i + 1) * rows, :at] = factor[...]
    out[:, at : at + other.shape[1]] = other[...]
    at += other.shape[1]
    for first in range(0, low.shape[0], tokens):
        out[:, at : at + LANES] = low[first : first + tokens, :].astype(BF16)
        at += LANES


def to_trade(place, factors, other, low, half):
    tokens = other.shape[0]
    width = half + other.shape[1] + low.shape[0] // tokens * LANES
    fixed = lambda one: pl.BlockSpec(one.shape, lambda i, s: (0, 0))
    return pl.pallas_call(
        trade_kernel,
        grid_spec=pltpu.PrefetchScalarGridSpec(
            num_scalar_prefetch=1,
            grid=(1,),
            in_specs=[pl.BlockSpec((one.shape[0], half), lambda i, s: (0, s[0])) for one in factors]
            + [fixed(other), fixed(low)],
            out_specs=pl.BlockSpec((tokens, width), lambda i, s: (0, 0)),
        ),
        out_shape=jax.ShapeDtypeStruct((tokens, width), BF16),
        compiler_params=pltpu.CompilerParams(vmem_limit_bytes=24 * 2**20),
        cost_estimate=SMALL,
    )(jnp.asarray(place, jnp.int32).reshape(1), *factors, other, low)


def input_gradient_kernel(sources, shards, factor_blocks, scalars, *refs):
    weights, refs = refs[:shards], refs[shards:]
    factors, refs = refs[:factor_blocks], refs[factor_blocks:]
    wides, grads, outs = refs[:sources], refs[sources : 2 * sources], refs[-sources:]
    width = weights[0].shape[1]
    rows = jnp.concatenate([factor[...] for factor in factors], axis=0)
    every = jnp.concatenate([weight[...] for weight in weights], axis=1)
    places = [pl.ds(pl.multiple_of(scalars[k] * width, width), width) for k in range(shards)]
    for at in range(sources):
        ours = jnp.concatenate([grads[at][:, columns] for columns in places], axis=1)
        total = lax.dot_general(ours, every, TRANS_B, preferred_element_type=F32)
        total += jnp.dot(wides[at][...], rows, preferred_element_type=F32)
        outs[at][...] = total.astype(BF16)


def input_gradient_part(part, inner, whose, rows, grads, weights, wides, factors, halves, so_far):
    features = factors[0].shape[1]
    sources, shards, tokens = len(grads), len(weights), grads[0].shape[0]
    width = weights[0].shape[1]
    block = min(rows, 512)
    steps = rows // block
    scalars = jnp.stack([*whose, part, inner]).astype(jnp.int32)
    in_specs = [pl.BlockSpec((block, width), lambda j, s: (s[shards] * steps + j, 0))]
    in_specs += [pl.BlockSpec((block, width), lambda j, s: (j, 0)) for _ in range(shards - 1)]
    in_specs += [
        pl.BlockSpec((one.shape[0], block), lambda j, s: (0, s[shards] * steps + j)) for one in factors
    ]
    in_specs += [
        pl.BlockSpec((one.shape[0], block), lambda j, s: (0, s[shards + 1] * steps + j)) for one in halves
    ]
    in_specs += [pl.BlockSpec(memory_space=pltpu.VMEM)] * (2 * sources)
    operands = [scalars, *weights, *factors, *halves, *wides, *grads]
    aliases = {}
    if so_far is not None:
        in_specs.append(pl.BlockSpec(memory_space=pl.ANY))
        operands.append(so_far)
        aliases = {len(operands) - 1: 0}
    return pl.pallas_call(
        functools.partial(input_gradient_kernel, sources, shards, len(factors) + len(halves)),
        grid_spec=pltpu.PrefetchScalarGridSpec(
            num_scalar_prefetch=1,
            grid=(steps,),
            in_specs=in_specs,
            out_specs=[pl.BlockSpec((tokens, block), lambda j, s: (0, s[shards] * steps + j))]
            + [pl.BlockSpec((tokens, block), lambda j, s: (0, j))] * (sources - 1),
        ),
        out_shape=[jax.ShapeDtypeStruct((tokens, features), BF16)]
        + [jax.ShapeDtypeStruct((tokens, rows), BF16)] * (sources - 1),
        input_output_aliases=aliases,
        compiler_params=pltpu.CompilerParams(vmem_limit_bytes=51 * 2**20),
        cost_estimate=SMALL,
    )(*operands)


def local(activations, output_gradient, base_weight, factor_down, factor_up, counts, owners):
    tokens, features = activations.shape
    columns = output_gradient.shape[1]
    own_slots, rank = factor_down.shape[:2]
    slots = owners.shape[0]
    n, subs, groups = lax.axis_size("fsdp"), lax.axis_size("sub"), lax.axis_size("groups")
    z, sub, y = lax.axis_index("fsdp"), lax.axis_index("sub"), lax.axis_index("groups")
    own_rows = own_slots * rank
    other_core = [(i, (i + 1) % subs) for i in range(subs)]

    both = range(subs)
    events = []

    def event(*arrays, cost=SMALL):
        events.append(mark(cost, *arrays, *events[-1:]))
        return events[-1]

    half = features // subs
    copies = groups * subs
    part_rows, width = base_weight.shape[0] // copies, base_weight.shape[1]

    def line_on(ups, downs, step, *earlier):
        if step < n:
            one, two = line_step(after(ups[-1], *earlier), after(downs[-1], *earlier), step)
            ups.append(one)
            downs.append(two)

    g_cores = over_cores(output_gradient)
    count_cores = over_cores(counts[0])
    x_cores = over_cores(activations)
    factors = [factor_down.reshape(own_rows, features)]

    def factor_on(*earlier):
        if len(factors) < n:
            factors.append(lax.ppermute(after(factors[-1], *earlier), "fsdp", around("fsdp")))

    up_here = factor_up.reshape(own_rows, columns)
    up_line = [up_here] + [
        lax.ppermute(up_here, "fsdp", [(i, (i + far) % n) for i in range(n)]) for far in range(1, n)
    ]

    if lax.axis_size("tp") == 2:
        tp_other = lax.ppermute(output_gradient, "tp", around("tp"))
        first = lax.axis_index("tp") == 0

        def whole_grad(one, two):
            return jnp.concatenate([jnp.where(first, one, two), jnp.where(first, two, one)], axis=1)
    else:
        tp_other = lax.all_gather(output_gradient, "tp", axis=1, tiled=True)

        def whole_grad(one, two):
            return two

    hot = owners[:, None] == lax.broadcasted_iota(jnp.int32, (slots, slots), 1)
    bounds = []
    for count in count_cores:
        seg_ends = jnp.cumsum(count)
        starts = jnp.sum(jnp.where(hot, (seg_ends - count)[:, None], 0), axis=0)
        ends = jnp.sum(jnp.where(hot, seg_ends[:, None], 0), axis=0)
        bounds.append((starts, ends))

    def ranges(devices):
        which = jnp.concatenate(
            [(at * subs + core) * own_slots + jnp.arange(own_slots, dtype=jnp.int32) for at, core in devices]
        )
        which = jnp.repeat(which, rank)
        found = which[:, None] == jnp.arange(slots, dtype=jnp.int32)[None, :]
        return tuple(
            jnp.stack([jnp.sum(jnp.where(found, one[end][None, :], 0), axis=1) for one in bounds])
            for end in range(2)
        )

    along_line = ranges([((z - j) % n, sub) for j in range(n)])
    weight_here = lax.dynamic_index_in_dim(
        base_weight.reshape(copies, part_rows, width), sub * groups + y, 0, keepdims=False
    )
    w_up, w_down = [weight_here], [weight_here]
    came = event(*up_line[1:], *g_cores[1:], *x_cores[1:], *along_line, weight_here, tp_other)

    line_on(w_up, w_down, 1, came)
    factor_on(came)
    low_back = low_rank([after(g_cores[0], came), *g_cores[1:]], up_line, *along_line, rank)
    low_back = sum_over_tp(adapter_scale_factor * low_back)
    down_blocks = outer(low_back, *along_line, x_cores, 1.0, n)
    own_grad = whole_grad(output_gradient, tp_other)
    came = event(factors[-1], cost=LONG)
    factor_on(came)
    came = event(w_up[1], w_down[1], own_grad)

    weight_arrivals, whose = [], [z] + [arrival_owner(step) for step in range(1, n)]

    def weight_arrives(step, *earlier):
        mine = [after(arrival(w_up, w_down, step), *earlier)]
        for _ in range(1, groups):
            mine.append(lax.ppermute(mine[-1], "groups", around("groups")))
        weight_arrivals.append(mine)

    def to_sum(step):
        lower, upper = down_blocks[n - step], down_blocks[step]
        if step > 1:
            lower = (lower.astype(F32) + from_above.astype(F32)).astype(BF16)
            upper = (upper.astype(F32) + from_below.astype(F32)).astype(BF16)
        elif n >= 4:
            lower = upper = jnp.where(z == 0, upper, lower)
        return lower, upper

    def sum_on(step, lower, upper, *earlier):
        lower, upper = after(lower, *earlier), after(upper, *earlier)
        if step == 1 and n >= 4:
            got = lax.ppermute(lower, "fsdp", [(n - 1, n - 2), (0, 1)])
            return got, got
        return (
            lax.ppermute(lower, "fsdp", [(i, i - 1) for i in range(n - step, n)]),
            lax.ppermute(upper, "fsdp", [(i, i + 1) for i in range(step)]),
        )

    from_above = from_below = low_in = None
    early = min(n, 3)
    if early * own_rows % LANES:
        early = 0
    for step in range(2, n):
        line_on(w_up, w_down, step, came)
        from_above, from_below = sum_on(step - 1, *to_sum(step - 1), came)
        weight_arrives(step - 1, came)
        if step == n - 1 and early:
            low_in = low_rank(
                [after(x_cores[0], came), *x_cores[1:]],
                factors[:early],
                *ranges([((z - j) % n, sub) for j in range(early)]),
                rank,
            )
        factor_on(event(factors[-1], cost=LONG))
        if step == n - 1:
            low_in = low_rank(
                x_cores, factors[early:], *ranges([((z - j) % n, sub) for j in range(early, n)]), rank, low_in
            )
            low_in = sum_over_tp(low_in)
            came = event(low_in)
        came = event(w_up[-1], w_down[-1], from_above, from_below, *weight_arrivals[-1][1:])

    traded = [None]
    for b in range(1, subs):
        there = to_trade((sub + b) % subs, factors, tp_other, low_back, half)
        there = lax.ppermute(after(there, came), "sub", [(i, (i + b) % subs) for i in range(subs)])
        traded.append((there, there[:, half:]))
    low_back_all, tp_cores = low_back, [tp_other]
    cut = tp_other.shape[1]
    for b in range(1, subs):
        rest = traded[b][1]
        tp_cores.append(rest[:, :cut])
        theirs = [rest[:, cut + at * LANES : cut + (at + 1) * LANES] for at in both]
        theirs = jnp.concatenate([theirs[(at - b) % subs] for at in both], axis=0)
        low_back_all = low_back_all + theirs.astype(F32)
    grads = [own_grad] + [whole_grad(one, two) for one, two in zip(g_cores[1:], tp_cores[1:], strict=True)]
    wides = spread_out(
        low_back_all + came[:1], *ranges([((z - j) % n, (sub - b) % subs) for b in both for j in range(n)])
    )

    def ig(a, so_far, others):
        inner = (y - a) % groups
        so_far, *for_others = input_gradient_part(
            sub * groups + inner,
            inner,
            whose,
            part_rows,
            grads,
            [base_weight] + [arrived[a] for arrived in weight_arrivals],
            wides,
            factors,
            [one[0] for one in traded[1:]],
            so_far,
        )
        return so_far, [*others, for_others]

    if n > 2:
        from_above, from_below = sum_on(n - 1, *to_sum(n - 1), came)
        weight_arrives(n - 1, came)
    grad_down = down_blocks[0] + from_above.astype(F32) + from_below.astype(F32)

    bits = n.bit_length() - 1
    turned = [sum(((place >> k) & 1) << (bits - 1 - k) for k in range(bits)) for place in range(n)]
    up_total, there = outer(
        low_in, *ranges([(z ^ place, sub) for place in turned]), g_cores, adapter_scale_factor, 2
    )
    input_gradient, others, last = None, [], [came]
    for bit in range(bits):
        if bit:
            there = up_total[up_total.shape[0] // 2 :].astype(BF16)
            up_total = up_total[: up_total.shape[0] // 2]
        if bit == 1:
            last += [from_above, from_below, *weight_arrivals[-1][1:]]
        got = lax.ppermute(after(there, *last), "fsdp", [(i, i ^ (1 << bit)) for i in range(n)])
        if not bit:
            got = after(got, *wides, *grads)
        if bit < bits - 1:
            up_total = up_total + got.astype(F32)
        if not bit:
            for a in range(groups):
                input_gradient, others = ig(a, input_gradient, others)
            last = [came, input_gradient]

    round_4 = [from_above, from_below, input_gradient]
    for a in range(groups):
        for b, one in enumerate(others[a], 1):
            theirs = lax.ppermute(
                after(one, *round_4), "sub", [(i, (i - b) % subs) for i in range(subs)]
            )
            part = ((sub + b) % subs) * groups + (y - a) % groups
            input_gradient = lax.dynamic_update_slice_in_dim(
                input_gradient, theirs, part * part_rows, axis=1
            )
    up_total = up_total + after(got, input_gradient).astype(F32)
    return (
        input_gradient,
        grad_down.reshape(own_slots, rank, features),
        up_total.reshape(own_slots, rank, columns),
    )


def solution(mesh):
    placed = (
        P(("groups", "fsdp", "sub"), "tp"),
        P(("groups", "fsdp", "sub"), "tp"),
        P("tp", "fsdp"),
        P(("groups", "fsdp", "sub"), None, "tp"),
        P(("groups", "fsdp", "sub"), None, "tp"),
        P(("groups", "fsdp", "sub"), None),
        P("groups"),
    )
    return jax.shard_map(
        local,
        mesh=mesh,
        in_specs=placed,
        out_specs=(
            P(("groups", "fsdp", "sub"), "tp"),
            P(("groups", "fsdp", "sub"), None, "tp"),
            P(("groups", "fsdp", "sub"), None, "tp"),
        ),
        check_vma=False,
    )
```

```python
import functools

import jax
import jax.numpy as jnp
from jax import lax
from jax.experimental import pallas as pl
from jax.experimental.pallas import tpu as pltpu
from jax.sharding import PartitionSpec as P

adapter_scale_factor = 0.25
F32 = jnp.float32
BF16 = jnp.bfloat16
LANES = 128
PIECES = 1
TRANS_B = (((1,), (1,)), ((), ()))
SMALL = pl.CostEstimate(flops=1, bytes_accessed=1, transcendentals=0)
LONG = pl.CostEstimate(flops=20 * 10**9, bytes_accessed=1, transcendentals=0)
TRANS_A = (((0,), (0,)), ((), ()))


def after(value, *earlier):
    return lax.optimization_barrier((value, *earlier))[0]


def mark_kernel(*refs):
    refs[-1][...] = jnp.zeros_like(refs[-1])


def mark(cost, *arrays):
    return pl.pallas_call(
        mark_kernel,
        in_specs=[pl.BlockSpec(memory_space=pl.ANY) for _ in arrays],
        out_shape=jax.ShapeDtypeStruct((8, LANES), F32),
        compiler_params=pltpu.CompilerParams(vmem_limit_bytes=2**20),
        cost_estimate=cost,
    )(*arrays)


def around(axis):
    count = lax.axis_size(axis)
    return [(i, (i + 1) % count) for i in range(count)]


def line_step(up, down, step):
    count, at = lax.axis_size("fsdp"), lax.axis_index("fsdp")
    if step == count - 1 and count >= 4:
        both = lax.ppermute(
            jnp.where(at == 1, down, up), "fsdp", [(count - 2, count - 1), (1, 0)]
        )
        return both, both
    return (
        lax.ppermute(up, "fsdp", [(i, i + 1) for i in range(step - 1, count - 1)]),
        lax.ppermute(down, "fsdp", [(i, i - 1) for i in range(1, count - step + 1)]),
    )


def arrives(step, place):
    count = lax.axis_size("fsdp")
    if 2 * place >= count:
        return (True, step) if step <= place else (False, step - place)
    room = count - 1 - place
    return (False, step) if step <= room else (True, step - room)


def arrival(up, down, step):
    count, at = lax.axis_size("fsdp"), lax.axis_index("fsdp")
    choices = {}
    for place in range(count):
        choices.setdefault(arrives(step, place), []).append(place)
    pick = None
    for (from_up, far), places in choices.items():
        one = up[far] if from_up else down[far]
        here = functools.reduce(jnp.logical_or, [at == place for place in places])
        pick = one if pick is None else jnp.where(here, one, pick)
    return pick


def arrival_owner(step):
    count, at = lax.axis_size("fsdp"), lax.axis_index("fsdp")
    owner = 0
    for place in range(count):
        from_up, far = arrives(step, place)
        owner = jnp.where(at == place, place - far if from_up else place + far, owner)
    return owner


def sum_over_tp(part):
    if lax.axis_size("tp") == 2:
        return part + lax.ppermute(part.astype(BF16), "tp", around("tp")).astype(F32)
    return lax.psum(part.astype(BF16), "tp").astype(F32)


def over_cores(one):
    every = [one]
    for _ in range(1, lax.axis_size("sub")):
        every.append(lax.ppermute(every[-1], "sub", around("sub")))
    return every


def in_range(start, end, at, tokens):
    start, end = start[at : at + 1, :], end[at : at + 1, :]
    position = lax.broadcasted_iota(jnp.int32, (tokens, start.shape[1]), 0)
    return (position >= start) & (position < end)


def row_pieces(xs, chunk):
    rows = xs[0].shape[0] // PIECES
    one = lambda piece: pl.BlockSpec((rows, chunk), lambda k: (piece, k))
    return [one(piece) for _ in xs for piece in range(PIECES)]


def low_kernel(sources, count, rank, with_prior, *refs):
    xs, refs = refs[: sources * PIECES], refs[sources * PIECES :]
    blocks, (start, end), refs = refs[:count], refs[count : count + 2], refs[count + 2 :]
    prior = refs[0] if with_prior else None
    out, total = refs[-2:]
    piece = xs[0].shape[0]
    tokens = piece * PIECES
    step = pl.program_id(0)
    rows = jnp.concatenate([block[...] for block in blocks], axis=0)
    for at, x in enumerate(xs):
        here = pl.ds(at * piece, piece)
        part = lax.dot_general(x[...], rows, TRANS_B, preferred_element_type=F32)

        @pl.when(step == 0)
        def _():
            total[here, :] = part

        @pl.when(step > 0)
        def _():
            total[here, :] += part

    @pl.when(step == pl.num_programs(0) - 1)
    def _():
        for at in range(sources):
            here = pl.ds(at * tokens, tokens)
            chosen = jnp.where(in_range(start, end, at, tokens), total[here, :], 0.0)
            low = chosen[:, :LANES]
            for lane in range(LANES, chosen.shape[1], LANES):
                low = low + chosen[:, lane : lane + LANES]
            turn = LANES // 2
            while turn >= rank:
                low = low + pltpu.roll(low, turn, 1)
                turn //= 2
            out[here, :] = low + prior[here, :] if with_prior else low


def low_rank(xs, blocks, start, end, rank, prior=None):
    tokens, depth = xs[0].shape
    chunk = min(depth, 1024)
    columns = start.shape[1]
    rows = len(xs) * tokens
    fixed = lambda shape: pl.BlockSpec(shape, lambda k: (0, 0))
    operands = [x for x in xs for _ in range(PIECES)]
    operands += [*blocks, start, end] + ([] if prior is None else [prior])
    in_specs = row_pieces(xs, chunk)
    in_specs += [pl.BlockSpec((b.shape[0], chunk), lambda k: (0, k)) for b in blocks]
    in_specs += [fixed(start.shape), fixed(end.shape)]
    if prior is not None:
        in_specs.append(fixed((rows, LANES)))
    return pl.pallas_call(
        functools.partial(low_kernel, len(xs), len(blocks), rank, prior is not None),
        grid=(depth // chunk,),
        in_specs=in_specs,
        out_specs=fixed((rows, LANES)),
        out_shape=jax.ShapeDtypeStruct((rows, LANES), F32),
        scratch_shapes=[pltpu.VMEM((rows, columns), F32)],
        compiler_params=pltpu.CompilerParams(vmem_limit_bytes=20 * 2**20),
        cost_estimate=SMALL,
    )(*operands)


def spread(low, start, end, at):
    tokens, columns = low.shape[0], start.shape[1]
    repeated = jnp.concatenate([low] * (columns // LANES), axis=1)
    return jnp.where(in_range(start, end, at, tokens), repeated, 0.0).astype(BF16)


def spread_kernel(low, start, end, *outs):
    tokens = outs[0].shape[0]
    for at, out in enumerate(outs):
        out[...] = spread(low[pl.ds(at * tokens, tokens), :], start, end, at)


def spread_out(low, start, end):
    sources, columns = start.shape
    return pl.pallas_call(
        spread_kernel,
        out_shape=[jax.ShapeDtypeStruct((low.shape[0] // sources, columns), BF16)] * sources,
        compiler_params=pltpu.CompilerParams(vmem_limit_bytes=24 * 2**20),
        cost_estimate=SMALL,
    )(low, start, end)


def outer_kernel(scale, parts, low, start, end, *refs):
    xs, outs, wide = refs[: -1 - parts], refs[-1 - parts : -1], refs[-1]
    sources = len(xs) // PIECES
    tokens = low.shape[0] // sources

    @pl.when(pl.program_id(0) == 0)
    def _():
        for at in range(sources):
            here = pl.ds(at * tokens, tokens)
            wide[here, :] = spread(low[here, :], start, end, at)

    every = jnp.concatenate([x[...] for x in xs], axis=0)
    total = lax.dot_general(wide[...], every, TRANS_A, preferred_element_type=F32)
    if scale != 1.0:
        total = total * scale
    rows = total.shape[0] // parts
    for at, out in enumerate(outs):
        out[...] = total[at * rows : (at + 1) * rows].astype(out.dtype)


def outer(low, start, end, xs, scale, parts):
    tokens, features = xs[0].shape
    columns = start.shape[1]
    rows = columns // parts
    chunk = min(features, 512)
    fixed = lambda shape: pl.BlockSpec(shape, lambda k: (0, 0))
    moving = lambda count: pl.BlockSpec((count, chunk), lambda k: (0, k))
    return pl.pallas_call(
        functools.partial(outer_kernel, scale, parts),
        grid=(features // chunk,),
        in_specs=[fixed(low.shape), fixed(start.shape), fixed(end.shape)] + row_pieces(xs, chunk),
        out_specs=[moving(rows)] * parts,
        out_shape=[
            jax.ShapeDtypeStruct((rows, features), F32 if at == 0 else BF16) for at in range(parts)
        ],
        scratch_shapes=[pltpu.VMEM((len(xs) * tokens, columns), BF16)],
        compiler_params=pltpu.CompilerParams(vmem_limit_bytes=20 * 2**20),
        cost_estimate=SMALL,
    )(low, start, end, *[x for x in xs for _ in range(PIECES)])


def trade_kernel(_, *refs):
    *factors, other, low, out = refs
    tokens, at = out.shape[0], factors[0].shape[1]
    rows = factors[0].shape[0]
    for i, factor in enumerate(factors):
        out[i * rows : (i + 1) * rows, :at] = factor[...]
    out[:, at : at + other.shape[1]] = other[...]
    at += other.shape[1]
    for first in range(0, low.shape[0], tokens):
        out[:, at : at + LANES] = low[first : first + tokens, :].astype(BF16)
        at += LANES


def to_trade(place, factors, other, low, half):
    tokens = other.shape[0]
    width = half + other.shape[1] + low.shape[0] // tokens * LANES
    fixed = lambda one: pl.BlockSpec(one.shape, lambda i, s: (0, 0))
    return pl.pallas_call(
        trade_kernel,
        grid_spec=pltpu.PrefetchScalarGridSpec(
            num_scalar_prefetch=1,
            grid=(1,),
            in_specs=[pl.BlockSpec((one.shape[0], half), lambda i, s: (0, s[0])) for one in factors]
            + [fixed(other), fixed(low)],
            out_specs=pl.BlockSpec((tokens, width), lambda i, s: (0, 0)),
        ),
        out_shape=jax.ShapeDtypeStruct((tokens, width), BF16),
        compiler_params=pltpu.CompilerParams(vmem_limit_bytes=24 * 2**20),
        cost_estimate=SMALL,
    )(jnp.asarray(place, jnp.int32).reshape(1), *factors, other, low)


def input_gradient_kernel(sources, shards, factor_blocks, scalars, *refs):
    weights, refs = refs[:shards], refs[shards:]
    factors, refs = refs[:factor_blocks], refs[factor_blocks:]
    wides, grads, outs = refs[:sources], refs[sources : 2 * sources], refs[-sources:]
    width = weights[0].shape[1]
    rows = jnp.concatenate([factor[...] for factor in factors], axis=0)
    every = jnp.concatenate([weight[...] for weight in weights], axis=1)
    places = [pl.ds(pl.multiple_of(scalars[k] * width, width), width) for k in range(shards)]
    for at in range(sources):
        ours = jnp.concatenate([grads[at][:, columns] for columns in places], axis=1)
        total = lax.dot_general(ours, every, TRANS_B, preferred_element_type=F32)
        total += jnp.dot(wides[at][...], rows, preferred_element_type=F32)
        outs[at][...] = total.astype(BF16)


def input_gradient_part(part, inner, whose, rows, grads, weights, wides, factors, halves, so_far):
    features = factors[0].shape[1]
    sources, shards, tokens = len(grads), len(weights), grads[0].shape[0]
    width = weights[0].shape[1]
    block = min(rows, 512)
    steps = rows // block
    scalars = jnp.stack([*whose, part, inner]).astype(jnp.int32)
    in_specs = [pl.BlockSpec((block, width), lambda j, s: (s[shards] * steps + j, 0))]
    in_specs += [pl.BlockSpec((block, width), lambda j, s: (j, 0)) for _ in range(shards - 1)]
    in_specs += [
        pl.BlockSpec((one.shape[0], block), lambda j, s: (0, s[shards] * steps + j)) for one in factors
    ]
    in_specs += [
        pl.BlockSpec((one.shape[0], block), lambda j, s: (0, s[shards + 1] * steps + j)) for one in halves
    ]
    in_specs += [pl.BlockSpec(memory_space=pltpu.VMEM)] * (2 * sources)
    operands = [scalars, *weights, *factors, *halves, *wides, *grads]
    aliases = {}
    if so_far is not None:
        in_specs.append(pl.BlockSpec(memory_space=pl.ANY))
        operands.append(so_far)
        aliases = {len(operands) - 1: 0}
    return pl.pallas_call(
        functools.partial(input_gradient_kernel, sources, shards, len(factors) + len(halves)),
        grid_spec=pltpu.PrefetchScalarGridSpec(
            num_scalar_prefetch=1,
            grid=(steps,),
            in_specs=in_specs,
            out_specs=[pl.BlockSpec((tokens, block), lambda j, s: (0, s[shards] * steps + j))]
            + [pl.BlockSpec((tokens, block), lambda j, s: (0, j))] * (sources - 1),
        ),
        out_shape=[jax.ShapeDtypeStruct((tokens, features), BF16)]
        + [jax.ShapeDtypeStruct((tokens, rows), BF16)] * (sources - 1),
        input_output_aliases=aliases,
        compiler_params=pltpu.CompilerParams(vmem_limit_bytes=51 * 2**20),
        cost_estimate=SMALL,
    )(*operands)


def local(activations, output_gradient, base_weight, factor_down, factor_up, counts, owners):
    tokens, features = activations.shape
    columns = output_gradient.shape[1]
    own_slots, rank = factor_down.shape[:2]
    slots = owners.shape[0]
    n, subs, groups = lax.axis_size("fsdp"), lax.axis_size("sub"), lax.axis_size("groups")
    z, sub, y = lax.axis_index("fsdp"), lax.axis_index("sub"), lax.axis_index("groups")
    own_rows = own_slots * rank
    other_core = [(i, (i + 1) % subs) for i in range(subs)]

    both = range(subs)
    events = []

    def event(*arrays, cost=SMALL):
        events.append(mark(cost, *arrays, *events[-1:]))
        return events[-1]

    half = features // subs
    copies = groups * subs
    part_rows, width = base_weight.shape[0] // copies, base_weight.shape[1]

    def line_on(ups, downs, step, *earlier):
        if step < n:
            one, two = line_step(after(ups[-1], *earlier), after(downs[-1], *earlier), step)
            ups.append(one)
            downs.append(two)

    g_cores = over_cores(output_gradient)
    count_cores = over_cores(counts[0])
    x_cores = over_cores(activations)
    factors = [factor_down.reshape(own_rows, features)]

    def factor_on(*earlier):
        if len(factors) < n:
            factors.append(lax.ppermute(after(factors[-1], *earlier), "fsdp", around("fsdp")))

    up_here = factor_up.reshape(own_rows, columns)
    up_line = [up_here] + [
        lax.ppermute(up_here, "fsdp", [(i, (i + far) % n) for i in range(n)]) for far in range(1, n)
    ]

    hot = owners[:, None] == lax.broadcasted_iota(jnp.int32, (slots, slots), 1)
    bounds = []
    for count in count_cores:
        seg_ends = jnp.cumsum(count)
        starts = jnp.sum(jnp.where(hot, (seg_ends - count)[:, None], 0), axis=0)
        ends = jnp.sum(jnp.where(hot, seg_ends[:, None], 0), axis=0)
        bounds.append((starts, ends))

    def ranges(devices):
        which = jnp.concatenate(
            [(at * subs + core) * own_slots + jnp.arange(own_slots, dtype=jnp.int32) for at, core in devices]
        )
        which = jnp.repeat(which, rank)
        found = which[:, None] == jnp.arange(slots, dtype=jnp.int32)[None, :]
        return tuple(
            jnp.stack([jnp.sum(jnp.where(found, one[end][None, :], 0), axis=1) for one in bounds])
            for end in range(2)
        )

    along_line = ranges([((z - j) % n, sub) for j in range(n)])
    weight_here = lax.dynamic_index_in_dim(
        base_weight.reshape(copies, part_rows, width), sub * groups + y, 0, keepdims=False
    )
    w_up, w_down = [weight_here], [weight_here]
    came = event(*up_line[1:], *g_cores[1:], *x_cores[1:], *along_line, weight_here)

    line_on(w_up, w_down, 1, came)
    factor_on(came)
    low_back = low_rank([after(g_cores[0], came), *g_cores[1:]], up_line, *along_line, rank)
    low_back = sum_over_tp(adapter_scale_factor * low_back)
    if lax.axis_size("tp") == 2:
        tp_other = lax.ppermute(after(output_gradient, low_back), "tp", around("tp"))
        first = lax.axis_index("tp") == 0

        def whole_grad(one, two):
            return jnp.concatenate([jnp.where(first, one, two), jnp.where(first, two, one)], axis=1)
    else:
        tp_other = lax.all_gather(output_gradient, "tp", axis=1, tiled=True)

        def whole_grad(one, two):
            return two

    down_blocks = outer(low_back, *along_line, x_cores, 1.0, n)
    own_grad = whole_grad(output_gradient, tp_other)
    came = event(factors[-1], cost=LONG)
    factor_on(came)
    came = event(w_up[1], w_down[1], tp_other)

    weight_arrivals, whose = [], [z] + [arrival_owner(step) for step in range(1, n)]

    def weight_arrives(step, *earlier):
        mine = [after(arrival(w_up, w_down, step), *earlier)]
        for _ in range(1, groups):
            mine.append(lax.ppermute(mine[-1], "groups", around("groups")))
        weight_arrivals.append(mine)

    def to_sum(step):
        lower, upper = down_blocks[n - step], down_blocks[step]
        if step > 1:
            lower = (lower.astype(F32) + from_above.astype(F32)).astype(BF16)
            upper = (upper.astype(F32) + from_below.astype(F32)).astype(BF16)
        elif n >= 4:
            lower = upper = jnp.where(z == 0, upper, lower)
        return lower, upper

    def sum_on(step, lower, upper, *earlier):
        lower, upper = after(lower, *earlier), after(upper, *earlier)
        if step == 1 and n >= 4:
            got = lax.ppermute(lower, "fsdp", [(n - 1, n - 2), (0, 1)])
            return got, got
        return (
            lax.ppermute(lower, "fsdp", [(i, i - 1) for i in range(n - step, n)]),
            lax.ppermute(upper, "fsdp", [(i, i + 1) for i in range(step)]),
        )

    from_above = from_below = low_in = None
    early = min(n, 3)
    if early * own_rows % LANES:
        early = 0
    for step in range(2, n):
        line_on(w_up, w_down, step, came)
        from_above, from_below = sum_on(step - 1, *to_sum(step - 1), came)
        weight_arrives(step - 1, came)
        if step == n - 1 and early:
            low_in = low_rank(
                [after(x_cores[0], came), *x_cores[1:]],
                factors[:early],
                *ranges([((z - j) % n, sub) for j in range(early)]),
                rank,
            )
        factor_on(event(factors[-1], cost=LONG))
        if step == n - 1:
            low_in = low_rank(
                x_cores, factors[early:], *ranges([((z - j) % n, sub) for j in range(early, n)]), rank, low_in
            )
            low_in = sum_over_tp(low_in)
            came = event(low_in)
        came = event(w_up[-1], w_down[-1], from_above, from_below, *weight_arrivals[-1][1:])

    traded = [None]
    for b in range(1, subs):
        there = to_trade((sub + b) % subs, factors, tp_other, low_back, half)
        there = lax.ppermute(after(there, came), "sub", [(i, (i + b) % subs) for i in range(subs)])
        traded.append((there, there[:, half:]))
    low_back_all, tp_cores = low_back, [tp_other]
    cut = tp_other.shape[1]
    for b in range(1, subs):
        rest = traded[b][1]
        tp_cores.append(rest[:, :cut])
        theirs = [rest[:, cut + at * LANES : cut + (at + 1) * LANES] for at in both]
        theirs = jnp.concatenate([theirs[(at - b) % subs] for at in both], axis=0)
        low_back_all = low_back_all + theirs.astype(F32)
    grads = [own_grad] + [whole_grad(one, two) for one, two in zip(g_cores[1:], tp_cores[1:], strict=True)]
    wides = spread_out(
        low_back_all + came[:1], *ranges([((z - j) % n, (sub - b) % subs) for b in both for j in range(n)])
    )

    def ig(a, so_far, others):
        inner = (y - a) % groups
        so_far, *for_others = input_gradient_part(
            sub * groups + inner,
            inner,
            whose,
            part_rows,
            grads,
            [base_weight] + [arrived[a] for arrived in weight_arrivals],
            wides,
            factors,
            [one[0] for one in traded[1:]],
            so_far,
        )
        return so_far, [*others, for_others]

    if n > 2:
        from_above, from_below = sum_on(n - 1, *to_sum(n - 1), came)
        weight_arrives(n - 1, came)
    grad_down = down_blocks[0] + from_above.astype(F32) + from_below.astype(F32)

    bits = n.bit_length() - 1
    turned = [sum(((place >> k) & 1) << (bits - 1 - k) for k in range(bits)) for place in range(n)]
    up_total, there = outer(
        low_in, *ranges([(z ^ place, sub) for place in turned]), g_cores, adapter_scale_factor, 2
    )
    input_gradient, others, last = None, [], [came]
    for bit in range(bits):
        if bit:
            there = up_total[up_total.shape[0] // 2 :].astype(BF16)
            up_total = up_total[: up_total.shape[0] // 2]
        if bit == 1:
            last += [from_above, from_below, *weight_arrivals[-1][1:]]
        got = lax.ppermute(after(there, *last), "fsdp", [(i, i ^ (1 << bit)) for i in range(n)])
        if not bit:
            got = after(got, *wides, *grads)
        if bit < bits - 1:
            up_total = up_total + got.astype(F32)
        if not bit:
            for a in range(groups):
                input_gradient, others = ig(a, input_gradient, others)
            last = [came, input_gradient]

    round_4 = [from_above, from_below, input_gradient]
    for a in range(groups):
        for b, one in enumerate(others[a], 1):
            theirs = lax.ppermute(
                after(one, *round_4), "sub", [(i, (i - b) % subs) for i in range(subs)]
            )
            part = ((sub + b) % subs) * groups + (y - a) % groups
            input_gradient = lax.dynamic_update_slice_in_dim(
                input_gradient, theirs, part * part_rows, axis=1
            )
    up_total = up_total + after(got, input_gradient).astype(F32)
    return (
        input_gradient,
        grad_down.reshape(own_slots, rank, features),
        up_total.reshape(own_slots, rank, columns),
    )


def solution(mesh):
    placed = (
        P(("groups", "fsdp", "sub"), "tp"),
        P(("groups", "fsdp", "sub"), "tp"),
        P("tp", "fsdp"),
        P(("groups", "fsdp", "sub"), None, "tp"),
        P(("groups", "fsdp", "sub"), None, "tp"),
        P(("groups", "fsdp", "sub"), None),
        P("groups"),
    )
    return jax.shard_map(
        local,
        mesh=mesh,
        in_specs=placed,
        out_specs=(
            P(("groups", "fsdp", "sub"), "tp"),
            P(("groups", "fsdp", "sub"), None, "tp"),
            P(("groups", "fsdp", "sub"), None, "tp"),
        ),
        check_vma=False,
    )
```
